128 devices in a mesh: dp: 32 (over y, x, core), tensor: 4 (over z).
Axes of the slice: x: 4, y: 4, z: 4, core: 2. Of those that a mesh axis runs over, the one named last changes fastest.
Arguments:
- residual: bfloat16 [2048, 4608], P(('dp', 'tensor')), may hold values from -5.4 to 5.4
- queries: bfloat16 [2048, 2560], P('dp', 'tensor'), may hold values from -30 to 30
- new_keys: bfloat16 [2048, 2560], P('dp', 'tensor'), may hold values from -6 to 6
- new_values: bfloat16 [2048, 2560], P('dp', 'tensor'), may hold values from -6 to 6
- cache_keys: bfloat16 [32768, 2560], P('dp', 'tensor'), may hold values from -6 to 6
- cache_values: bfloat16 [32768, 2560], P('dp', 'tensor'), may hold values from -6 to 6
- out_weight: bfloat16 [2560, 4608], P('tensor', 'dp'), may hold values from -0.125 to 0.125
- norm_gain: float32 [4608], replicated, may hold values from 0.1 to 1.9
- route_ids: int32 [2048, 2], P(('dp', 'tensor')), may hold values from 0 to 7, all different within a row; in each aligned block of 16 rows (0 to 15, 16 to 31, ...) at most 5 rows name the same one
- route_weight: float32 [2048, 2], P(('dp', 'tensor')), may hold values from 0.2 to 1
- gate_weight: bfloat16 [4608, 98304], P(None, ('dp', 'tensor')), may hold values from -0.09375 to 0.09375
- up_weight: bfloat16 [4608, 98304], P(None, ('dp', 'tensor')), may hold values from -0.09375 to 0.09375
- down_weight: bfloat16 [98304, 4608], P(('dp', 'tensor')), may hold values from -0.0546875 to 0.0546875
Outputs:
- layer_out: bfloat16 [2048, 4608], P(('dp', 'tensor'))
The draws below stay inside these ranges and needn't reach their ends.
Inputs may be any that keep to these rules, and one draw needn't show every extreme that they name: `route_ids`: within each aligned block of 16 rows (the tokens of one device of dp+tensor), no expert is named more than 5 times, a bound that some block reaches; the 2 experts of a row differ.
All inputs are finite; a program needn't handle non-finite values.
Results may differ from the reference program's by a relative error of at most 0.02055.
Values may be sent and summed in bfloat16 or wider, within the bound.
No kernel may reach another device: no remote copies, remote signals or barrier semaphores. Data moves between devices by JAX's collectives and lax.ppermute only.
A program may use at most 128 MiB of HBM per device.

```python
import math
import jax
import jax.numpy as jnp
import numpy as np
from jax import lax

D = 4608
H = 20
HD = 128
E = 8
FF = 12288
TOP = 2
Q_DEV = 64
TOKENS = 2048
CTX = 32768
HW = 2560
TOK_SRC = 16
CAP = 5
HID_DEV = 768
N_DP = 32


def draw_residual(key, part):
    key = jax.random.fold_in(key, 11)
    key_row, key_col, key_val = jax.random.split(key, 3)
    row_scale = jnp.exp(jax.random.uniform(key_row, (TOKENS, 1), jnp.float32, math.log(0.3), math.log(3.0)))
    col_scale = jnp.exp(jax.random.uniform(key_col, (1, D), jnp.float32, math.log(0.3), math.log(3.0)))
    values = jnp.clip(jax.random.normal(key_val, (TOKENS, D), jnp.float32), -6.0, 6.0)
    return (0.1 * row_scale * col_scale * values).astype(jnp.bfloat16)


def draw_queries(key, part):
    key = jax.random.fold_in(key, 12)
    key_base = jax.random.fold_in(key, 0)
    result = jnp.clip(2.5 * jax.random.normal(key_base, (TOKENS, H * HD), jnp.float32), -10.0, 10.0)
    return result.astype(jnp.bfloat16)


def draw_cache_keys(key, part):
    key = jax.random.fold_in(key, 13)
    result = jnp.clip(jax.random.normal(key, (CTX, H * HD), jnp.float32), -6.0, 6.0)
    return result.astype(jnp.bfloat16)


def levels(stream_key, shape, cuts, smallest, high):
    gain, own = 1.0, jax.random.fold_in(stream_key, 6)
    for position, shards_of in cuts:
        draws = jnp.exp(jax.random.uniform(jax.random.fold_in(own, position), (shards_of,), jnp.float32, smallest / len(cuts), high / len(cuts)))
        gain = gain * jnp.repeat(draws, shape[position] // shards_of).reshape([-1 if axis == position else 1 for axis in range(len(shape))])
    return gain


def deal_out(key, own, number, rows, amount, top, reach, skew):
    sequence = jax.random.permutation(key, amount)
    crowded, usual = portions_of(amount, rows * top, reach, skew, True), portions_of(amount, rows * top, reach, skew, False)
    places = jnp.arange(amount)

    def named(lengths, turn):
        used = int((lengths > 0).sum())
        fixed = max(1, used // 4)
        moved = fixed + (places - fixed + turn * (used - fixed)) % max(1, amount - fixed)
        return jnp.zeros((amount,), jnp.int32).at[sequence[jnp.where(places < fixed, places, moved)]].set(jnp.asarray(lengths, jnp.int32))

    lengths = jnp.where(number % 4 == 0, named(crowded, number // 4), named(usual, number - number // 4 - 1))
    mixed = jax.random.permutation(jax.random.fold_in(own, 3), amount)
    source_of, taker = mixed[0:amount // 2 * 2:2], mixed[1:amount // 2 * 2:2]
    room = jnp.minimum(lengths[source_of] - 1, reach - lengths[taker]) // 2
    room = jnp.where((source_of == sequence[0]) | (taker == sequence[0]) | (lengths[taker] == 0), 0, jnp.maximum(room, 0))
    moved = jax.random.randint(jax.random.fold_in(own, 4), (amount // 2,), 0, 1 << 20) % (room + 1)
    lengths = lengths.at[source_of].add(-moved).at[taker].add(moved)
    members = jnp.searchsorted(jnp.cumsum(lengths), jnp.arange(rows * top), side="right").astype(jnp.int32)
    grid = members.reshape(top, rows).T
    grid = grid[jax.random.permutation(jax.random.fold_in(own, 1), rows)]
    turn = jax.random.randint(jax.random.fold_in(own, 2), (rows, 1), 0, top)
    return jnp.take_along_axis(grid, (jnp.arange(top)[None, :] + turn) % top, axis=1)


def portions_of(amount, total, limit, slope, full):
    weights = [(1 << 20) // math.isqrt(grade ** slope) + 1 for grade in range(1, amount + 1)]
    largest = limit if full else min(limit, max(-(-total // amount), total * weights[0] // sum(weights)))
    least = 1 if total - largest >= amount - 1 else 0
    counts, surplus = [largest] + [least] * (amount - 1), total - largest - least * (amount - 1)
    while surplus > 0:
        candidates = [i for i in range(1, amount) if counts[i] < largest] or [i for i in range(1, amount) if counts[i] < limit]
        mass, left = sum([weights[i] for i in candidates]), surplus
        for i in candidates:
            addition = min(limit - counts[i], max(1, left * weights[i] // mass), surplus)
            counts[i] = counts[i] + addition
            surplus = surplus - addition
    return np.array(counts)


def bell_draw(stream_key, shape, deviation, reach, cuts=(), kind=jnp.bfloat16):
    array = deviation * jax.random.normal(stream_key, shape, jnp.float32)
    if cuts:
        array = array * levels(stream_key, shape, cuts, -0.22, 0.18)
    return jnp.clip(array, -reach, reach).astype(kind)


def setup_inputs(seed: int = 0) -> dict:
    splits = jax.random.split(jax.random.key(seed), 14)
    residual = draw_residual(jax.random.fold_in(splits[13], 71), 0)
    queries = draw_queries(jax.random.fold_in(splits[13], 71), 0)
    new_keys = bell_draw(splits[2], (TOKENS, HW), 1.0, 6.0, ((0, 32), (1, 4)))
    new_values = bell_draw(splits[3], (TOKENS, HW), 1.0, 6.0, ((0, 32), (1, 4)))
    cache_keys = draw_cache_keys(jax.random.fold_in(splits[13], 71), 0)
    cache_values = bell_draw(splits[5], (CTX, HW), 1.0, 6.0, ((0, 32), (1, 4)))
    out_weight = bell_draw(splits[6], (HW, D), HW ** -0.5, 0.125, ((0, 4), (1, 32)))
    norm_gain = jnp.clip(1.0 + 0.18 * jax.random.normal(splits[7], (D,), jnp.float32), 0.1, 1.9)
    route_ids_keys = jax.random.split(jax.random.fold_in(splits[8], 1), TOKENS // TOK_SRC)
    route_ids_turns = jax.random.permutation(jax.random.fold_in(splits[8], 3), TOKENS // TOK_SRC)
    route_ids = jax.vmap(lambda own, number: deal_out(jax.random.fold_in(splits[8], 2), own, number, TOK_SRC, E, TOP, CAP, 2))(route_ids_keys, route_ids_turns).reshape((TOKENS, TOP))
    route_weight = jnp.clip(0.2 + 0.8 * jax.random.uniform(splits[9], (TOKENS, TOP), jnp.float32) ** levels(splits[9], (TOKENS, TOP), ((0, 128),), -0.2, 0.2), 0.2, 1.0)
    gate_weight = bell_draw(splits[10], (D, E * FF), D ** -0.5, 0.09375, ((1, 128),))
    up_weight = bell_draw(splits[11], (D, E * FF), D ** -0.5, 0.09375, ((1, 128),))
    down_weight = bell_draw(splits[12], (E * FF, D), FF ** -0.5, 0.0546875, ((0, 128),))
    return {"residual": residual, "queries": queries, "new_keys": new_keys, "new_values": new_values, "cache_keys": cache_keys, "cache_values": cache_values, "out_weight": out_weight, "norm_gain": norm_gain, "route_ids": route_ids, "route_weight": route_weight, "gate_weight": gate_weight, "up_weight": up_weight, "down_weight": down_weight}


norm_eps = 1e-06

def attend_one(head_index, queries, all_keys, all_values):
    start_col = head_index * HD
    query_part = lax.dynamic_slice_in_dim(queries, start_col, HD, 1)
    key_part = lax.dynamic_slice_in_dim(all_keys, start_col, HD, 1)
    value_part = lax.dynamic_slice_in_dim(all_values, start_col, HD, 1)
    key_pos = jnp.arange(CTX + TOKENS, dtype=jnp.int32)
    query_blocks = query_part.reshape(N_DP, Q_DEV, HD)

    def one_block(args):
        block, block_index = args
        scores = jnp.dot(block, key_part.T, preferred_element_type=jnp.float32) * (1.0 / math.sqrt(HD))
        query_pos = CTX + block_index * Q_DEV + jnp.arange(Q_DEV, dtype=jnp.int32)
        allowed = key_pos[None, :] <= query_pos[:, None]
        scores = jnp.where(allowed, scores, -1e+30)
        row_max = lax.optimization_barrier(jnp.max(scores, axis=1, keepdims=True))
        weights = jnp.where(allowed, jnp.exp(scores - row_max), 0.0)
        weight_sum = lax.optimization_barrier(jnp.sum(weights, axis=1, keepdims=True))
        product = jnp.dot(weights.astype(jnp.bfloat16), value_part, preferred_element_type=jnp.float32)
        return product / weight_sum
    result = lax.map(one_block, (query_blocks, jnp.arange(N_DP, dtype=jnp.int32)))
    return result.reshape(TOKENS, HD)

def expert_output(expert, buffer, gate_weight, up_weight, down_weight):
    first_col = (expert * FF).astype(jnp.int32)
    gate_cols = lax.dynamic_slice_in_dim(gate_weight, first_col, FF, 1)
    up_cols = lax.dynamic_slice_in_dim(up_weight, first_col, FF, 1)
    down_rows = lax.dynamic_slice_in_dim(down_weight, first_col, FF, 0)
    gate_val = jnp.dot(buffer, gate_cols, preferred_element_type=jnp.float32)
    up_val = jnp.dot(buffer, up_cols, preferred_element_type=jnp.float32)
    hidden = (jax.nn.silu(gate_val) * up_val).astype(jnp.bfloat16)

    def add_share(share_index, acc_sum):
        first_unit = (jnp.asarray(share_index) * HID_DEV).astype(jnp.int32)
        hid_cols = lax.dynamic_slice_in_dim(hidden, first_unit, HID_DEV, 1)
        down_part = lax.dynamic_slice_in_dim(down_rows, first_unit, HID_DEV, 0)
        share_term = jnp.dot(hid_cols, down_part, preferred_element_type=jnp.float32).astype(jnp.bfloat16)
        share_term = lax.optimization_barrier(share_term)
        return acc_sum + share_term.astype(jnp.float32)
    return lax.fori_loop(0, FF // HID_DEV, add_share, jnp.zeros((buffer.shape[0], D), jnp.float32))

def reference(residual, queries, new_keys, new_values, cache_keys, cache_values, out_weight, norm_gain, route_ids, route_weight, gate_weight, up_weight, down_weight):
    all_keys = jnp.concatenate([cache_keys, new_keys], axis=0)
    all_values = jnp.concatenate([cache_values, new_values], axis=0)
    per_head = lax.map(lambda head_index: attend_one(head_index, queries, all_keys, all_values), jnp.arange(H, dtype=jnp.int32))
    attended = jnp.transpose(per_head, (1, 0, 2)).reshape(TOKENS, HW).astype(jnp.bfloat16)
    stream = (residual.astype(jnp.float32) + jnp.dot(attended, out_weight, preferred_element_type=jnp.float32)).astype(jnp.bfloat16)
    stream_f = stream.astype(jnp.float32)
    normed = (stream_f * lax.rsqrt(lax.optimization_barrier(jnp.mean(stream_f * stream_f, axis=1, keepdims=True)) + norm_eps) * norm_gain.astype(jnp.float32)).astype(jnp.bfloat16)
    blocks = TOKENS // TOK_SRC
    route_flat = route_ids.reshape(blocks, TOK_SRC * TOP).astype(jnp.int32)
    onehot = (route_flat[:, :, None] == jnp.arange(E, dtype=jnp.int32)[None, None, :]).astype(jnp.int32)
    before = (jnp.cumsum(onehot, axis=1) - onehot).astype(jnp.int32)
    slot_index = lax.optimization_barrier(jnp.sum(before * onehot, axis=2)).astype(jnp.int32)
    slot_rows = (jnp.arange(blocks, dtype=jnp.int32)[:, None] * CAP + slot_index).reshape(-1).astype(jnp.int32)
    route_list = route_flat.reshape(-1)
    route_token = jnp.arange(TOKENS * TOP, dtype=jnp.int32) // TOP
    route_gain = route_weight.reshape(-1).astype(jnp.float32)
    routed_rows = normed[route_token]
    buffer_rows = blocks * CAP

    def add_expert(expert, mixing):
        expert = jnp.asarray(expert).astype(jnp.int32)
        chosen = route_list == expert
        target = jnp.where(chosen, slot_rows, buffer_rows).astype(jnp.int32)
        buffer = jnp.zeros((buffer_rows, D), jnp.bfloat16).at[target].set(routed_rows, mode='drop')
        outputs = expert_output(expert, buffer, gate_weight, up_weight, down_weight)
        picked = outputs[jnp.where(chosen, slot_rows, 0).astype(jnp.int32)] * jnp.where(chosen, route_gain, 0.0)[:, None]
        return mixing + lax.optimization_barrier(jnp.sum(picked.reshape(TOKENS, TOP, D), axis=1))
    mixing = lax.fori_loop(0, E, add_expert, jnp.zeros((TOKENS, D), jnp.float32))
    return (stream_f + mixing).astype(jnp.bfloat16)
```

```python
import functools
import math

import jax
import jax.numpy as jnp
from jax import lax
from jax.experimental import pallas as pl
from jax.experimental.pallas import tpu as pltpu
from jax.sharding import Mesh, PartitionSpec as P

D = 4608
HD = 128
HEADS = 5
E = 8
TOP = 2
CAP = 5
NZ = 4
PLANE = 16
Q_DEV = 64
SLICE = D // NZ
ROWS = 24
USED = NZ * CAP
PACK = 128
WIDE = HEADS * HD + PACK
NORM_EPS = 1e-06
NEGATIVE = -1e30
TO_BASE2 = math.log2(math.e) / math.sqrt(HD)

XY = ("y", "xh", "xl")
ZXY = ("z", "y", "xh", "xl")
F32 = jnp.float32
BF16 = jnp.bfloat16


def params(mib):
    return pltpu.CompilerParams(vmem_limit_bytes=mib * 2**20)


def exchange(block, axes):
    return lax.all_to_all(block, axes, split_axis=0, concat_axis=0, tiled=True)


def other_core(block):
    return lax.ppermute(block, "c", [(0, 1), (1, 0)])


def three_parts(value):
    high = value.astype(BF16).astype(F32)
    rest = value - high
    middle = rest.astype(BF16).astype(F32)
    return high, middle, (rest - middle).astype(BF16).astype(F32)


def dot_nt(a, b, **kw):
    return lax.dot_general(a, b, (((1,), (1,)), ((), ())), preferred_element_type=F32, **kw)


def dot_nn(a, b, **kw):
    return lax.dot_general(a, b, (((1,), (0,)), ((), ())), preferred_element_type=F32, **kw)


Q_BLOCK = 256


def attend_kernel(place_ref, q_ref, ka_ref, kb_ref, na_ref, nb_ref, va_ref, vb_ref, wa_ref, wb_ref, out_ref):
    core, mine = place_ref[0], place_ref[1]
    row = lax.broadcasted_iota(jnp.int32, (Q_BLOCK, HD), 0)
    lane = lax.broadcasted_iota(jnp.int32, (Q_BLOCK, HD), 1)
    block = pl.program_id(0) * (Q_BLOCK // Q_DEV) + row // Q_DEV
    q_pos = (block * 2 + core) * Q_DEV + row % Q_DEV
    k_pos = jnp.where(lane < Q_DEV, mine * Q_DEV + lane, (mine + 1 - 2 * core) * Q_DEV + lane - Q_DEV)
    allowed = k_pos <= q_pos
    pack = jnp.zeros((Q_BLOCK, PACK), F32)
    for h in range(HEADS):
        cols = slice(h * HD, (h + 1) * HD)
        q = q_ref[:, cols]
        s1 = dot_nt(q, ka_ref[:, cols])
        s2 = dot_nt(q, kb_ref[:, cols])
        fresh = jnp.concatenate([na_ref[:, cols], nb_ref[:, cols]], axis=0)
        s3 = jnp.where(allowed, dot_nt(q, fresh), NEGATIVE)
        top = jnp.maximum(
            jnp.maximum(jnp.max(s1, axis=1, keepdims=True), jnp.max(s2, axis=1, keepdims=True)),
            jnp.max(s3, axis=1, keepdims=True),
        ) * TO_BASE2
        w1 = jnp.exp2(s1 * TO_BASE2 - top)
        w2 = jnp.exp2(s2 * TO_BASE2 - top)
        w3 = jnp.exp2(s3 * TO_BASE2 - top)
        total = (
            jnp.sum(w1, axis=1, keepdims=True)
            + jnp.sum(w2, axis=1, keepdims=True)
            + jnp.sum(w3, axis=1, keepdims=True)
        )
        fresh_v = jnp.concatenate([wa_ref[:, cols], wb_ref[:, cols]], axis=0)
        acc = (
            dot_nn(w1.astype(BF16), va_ref[:, cols])
            + dot_nn(w2.astype(BF16), vb_ref[:, cols])
            + dot_nn(w3.astype(BF16), fresh_v)
        )
        out_ref[:, cols] = (acc / total).astype(BF16)
        for part, value in enumerate(three_parts(top + jnp.log2(total))):
            pack = jnp.where(lane == part * 8 + h, value, pack)
    out_ref[:, HEADS * HD :] = pack.astype(BF16)


def attend(place, q, ka, kb, na, nb, va, vb, wa, wb):
    rows = q.shape[0]
    whole = lambda a: pl.BlockSpec(a.shape, lambda i: (0, 0))
    keys = (ka, kb, na, nb, va, vb, wa, wb)
    return pl.pallas_call(
        attend_kernel,
        grid=(rows // Q_BLOCK,),
        out_shape=jax.ShapeDtypeStruct((rows, WIDE), BF16),
        in_specs=[
            pl.BlockSpec(memory_space=pltpu.SMEM),
            pl.BlockSpec((Q_BLOCK, HEADS * HD), lambda i: (i, 0)),
            *[whole(a) for a in keys],
        ],
        out_specs=pl.BlockSpec((Q_BLOCK, WIDE), lambda i: (i, 0)),
        compiler_params=params(56),
        cost_estimate=pl.CostEstimate(flops=11 * 10**9, bytes_accessed=8 * 10**6, transcendentals=11 * 10**6),
        name="attend",
    )(place, q, *keys)


def project_kernel(parts_ref, weight_ref, out_ref, attended_ref):
    @pl.when(pl.program_id(0) == 0)
    def _():
        count = parts_ref.shape[0]
        sums = [
            parts_ref[i, :, HEADS * HD :].astype(F32) for i in range(count)
        ]
        for h in range(HEADS):
            cols = slice(h * HD, (h + 1) * HD)
            logs = [
                s[:, h : h + 1] + s[:, 8 + h : 9 + h] + s[:, 16 + h : 17 + h] for s in sums
            ]
            top = functools.reduce(jnp.maximum, logs)
            shares = [jnp.exp2(v - top) for v in logs]
            total = functools.reduce(jnp.add, shares)
            acc = functools.reduce(
                jnp.add, [shares[i] * parts_ref[i, :, cols].astype(F32) for i in range(count)]
            )
            attended_ref[:, cols] = (acc / total).astype(BF16)

    out_ref[0] = dot_nt(attended_ref[...], weight_ref[...]).astype(BF16)


def project(parts, weight):
    return pl.pallas_call(
        project_kernel,
        grid=(NZ,),
        out_shape=jax.ShapeDtypeStruct((NZ, Q_DEV, SLICE), BF16),
        in_specs=[
            pl.BlockSpec(parts.shape, lambda i: (0, 0, 0)),
            pl.BlockSpec((SLICE, HEADS * HD), lambda i: (i, 0)),
        ],
        out_specs=pl.BlockSpec((1, Q_DEV, SLICE), lambda i: (i, 0, 0)),
        scratch_shapes=[pltpu.VMEM((Q_DEV, HEADS * HD), BF16)],
        compiler_params=params(40),
        cost_estimate=pl.CostEstimate(flops=4 * 10**8, bytes_accessed=8 * 10**6, transcendentals=0),
        name="project",
    )(parts, weight)


def earlier():
    i = lax.broadcasted_iota(jnp.int32, (Q_DEV, Q_DEV), 0)
    j = lax.broadcasted_iota(jnp.int32, (Q_DEV, Q_DEV), 1)
    return i, j


def pack_kernel(heads_ref, residual_ref, gain_ref, routes_ref, stream_ref, packed_ref):
    total = residual_ref[...].astype(F32)
    summed = heads_ref[0].astype(F32)
    for z in range(1, NZ):
        summed = summed + heads_ref[z].astype(F32)
    stream = (total + summed).astype(BF16)
    stream_ref[...] = stream
    stream_f = stream.astype(F32)
    squares = stream_f * stream_f
    scaled = (stream_f * gain_ref[...]).astype(BF16)
    first, second = routes_ref[0:1, :], routes_ref[1:2, :]
    expert = lax.broadcasted_iota(jnp.int32, (E, Q_DEV), 0).astype(F32)
    hot0 = jnp.where(expert == first, 1.0, 0.0)
    hot1 = jnp.where(expert == second, 1.0, 0.0)
    j, i = earlier()
    before_t = jnp.where((j < i) & (j // 16 == i // 16), 1.0, 0.0)
    counts = dot_nn((hot0 + hot1).astype(BF16), before_t.astype(BF16))
    base = (lax.broadcasted_iota(jnp.int32, (1, Q_DEV), 1) // 16 * CAP).astype(F32)
    slot0 = jnp.sum(counts * hot0, axis=0, keepdims=True) + base
    slot1 = jnp.sum(counts * hot1, axis=0, keepdims=True) + base
    sums_row = dot_nt(jnp.ones((8, SLICE), F32), squares, precision=lax.Precision.HIGHEST)
    slot = lax.broadcasted_iota(jnp.int32, (HD, Q_DEV), 0).astype(F32)
    row = lax.broadcasted_iota(jnp.int32, (ROWS, HD), 0)
    for e in range(E):
        placing = jnp.where(
            ((slot == slot0) & (first == e)) | ((slot == slot1) & (second == e)), 1.0, 0.0
        )
        block = dot_nn(placing[:ROWS].astype(BF16), scaled)
        placed = dot_nt(sums_row, placing, precision=lax.Precision.HIGHEST)[0:1, :]
        high, middle, low = three_parts(placed)
        extra = jnp.where(
            row == USED, high, jnp.where(row == USED + 1, middle, jnp.where(row == USED + 2, low, 0.0))
        )
        packed_ref[e, :, :HD] = (block[:, :HD] + extra).astype(BF16)
        packed_ref[e, :, HD:] = block[:, HD:].astype(BF16)


def pack(heads, residual, gain, routes):
    return pl.pallas_call(
        pack_kernel,
        out_shape=(
            jax.ShapeDtypeStruct((Q_DEV, SLICE), BF16),
            jax.ShapeDtypeStruct((E, ROWS, SLICE), BF16),
        ),
        compiler_params=params(40),
        cost_estimate=pl.CostEstimate(flops=3 * 10**7, bytes_accessed=2 * 10**6, transcendentals=0),
        name="pack",
    )(heads, residual, gain, routes)


RCV = PLANE * ROWS
F_BLOCK = 256


def hidden_kernel(steps, x_ref, ga_ref, gb_ref, ua_ref, ub_ref, out_ref, scale_ref):
    step = pl.program_id(0)

    @pl.when(step == 0)
    def _():
        row = lax.broadcasted_iota(jnp.int32, (ROWS, HD), 0)
        lane = lax.broadcasted_iota(jnp.int32, (ROWS, HD), 1)
        for i in range(PLANE):
            part = x_ref[0, i * ROWS : (i + 1) * ROWS, :HD].astype(F32)
            for z in range(1, NZ):
                part = part + x_ref[z, i * ROWS : (i + 1) * ROWS, :HD].astype(F32)
            sums = jnp.sum(jnp.where((row >= USED) & (row < USED + 3), part, 0.0), axis=0, keepdims=True)
            column = jnp.sum(jnp.where((lane == row) & (row < USED), sums, 0.0), axis=1, keepdims=True)
            valid = lax.broadcasted_iota(jnp.int32, (ROWS, 1), 0) < USED
            scale_ref[i * ROWS : (i + 1) * ROWS, :] = jnp.broadcast_to(
                jnp.where(valid, lax.rsqrt(column * (1.0 / D) + NORM_EPS), 0.0), (ROWS, HD)
            )

    def work(gate_ref, up_ref):
        gate = jnp.zeros((RCV, F_BLOCK), F32)
        up = jnp.zeros((RCV, F_BLOCK), F32)
        for z in range(NZ):
            x = x_ref[z]
            gate = gate + dot_nn(x, gate_ref[z * SLICE : (z + 1) * SLICE, :])
            up = up + dot_nn(x, up_ref[z * SLICE : (z + 1) * SLICE, :])
        scale = scale_ref[:, :1]
        gate = gate * scale
        up = up * scale
        out_ref[...] = (gate / (1.0 + jnp.exp(-gate)) * up).astype(BF16)

    pl.when(step < steps)(lambda: work(ga_ref, ua_ref))
    pl.when(step >= steps)(lambda: work(gb_ref, ub_ref))


def hidden_units(x, ga, gb, ua, ub):
    steps = ga.shape[1] // F_BLOCK
    near = pl.BlockSpec((D, F_BLOCK), lambda i: (0, jnp.minimum(i, steps - 1)))
    far = pl.BlockSpec((D, F_BLOCK), lambda i: (0, jnp.maximum(i - steps, 0)))
    return pl.pallas_call(
        functools.partial(hidden_kernel, steps),
        grid=(2 * steps,),
        out_shape=jax.ShapeDtypeStruct((RCV, 2 * ga.shape[1]), BF16),
        in_specs=[pl.BlockSpec(x.shape, lambda i: (0, 0, 0)), near, far, near, far],
        out_specs=pl.BlockSpec((RCV, F_BLOCK), lambda i: (0, i)),
        scratch_shapes=[pltpu.VMEM((RCV, HD), F32)],
        compiler_params=params(56),
        cost_estimate=pl.CostEstimate(flops=11 * 10**9, bytes_accessed=33 * 10**6, transcendentals=10**6),
        name="hidden_units",
    )(x, ga, gb, ua, ub)


def down_kernel(h_ref, da_ref, db_ref, out_ref):
    half = da_ref.shape[0]
    out_ref[0] = (
        dot_nn(h_ref[:, :half], da_ref[...]) + dot_nn(h_ref[:, half:], db_ref[...])
    ).astype(BF16)


def down_units(h, da, db):
    part = pl.BlockSpec((da.shape[0], SLICE), lambda i: (0, i))
    return pl.pallas_call(
        down_kernel,
        grid=(NZ,),
        out_shape=jax.ShapeDtypeStruct((NZ, RCV, SLICE), BF16),
        in_specs=[pl.BlockSpec(h.shape, lambda i: (0, 0)), part, part],
        out_specs=pl.BlockSpec((1, RCV, SLICE), lambda i: (i, 0, 0)),
        compiler_params=params(48),
        cost_estimate=pl.CostEstimate(flops=55 * 10**8, bytes_accessed=20 * 10**6, transcendentals=0),
        name="down_units",
    )(h, da, db)


C_BLOCK = 384


def combine_kernel(returned_ref, stream_ref, routes_ref, out_ref, mix_ref):
    width = NZ * RCV

    @pl.when(pl.program_id(0) == 0)
    def _():
        first, second = routes_ref[:, 0:1], routes_ref[:, 1:2]
        weight0 = routes_ref[:, 2:3] + routes_ref[:, 3:4] + routes_ref[:, 4:5]
        weight1 = routes_ref[:, 5:6] + routes_ref[:, 6:7] + routes_ref[:, 7:8]
        expert = lax.broadcasted_iota(jnp.int32, (Q_DEV, HD), 1).astype(F32)
        hot0 = jnp.where(expert == first, 1.0, 0.0)
        hot1 = jnp.where(expert == second, 1.0, 0.0)
        i, j = earlier()
        before = jnp.where((j < i) & (j // 16 == i // 16), 1.0, 0.0)
        counts = dot_nn(before.astype(BF16), (hot0 + hot1).astype(BF16))
        base = (lax.broadcasted_iota(jnp.int32, (Q_DEV, 1), 0) // 16 * CAP).astype(F32)
        slot0 = jnp.sum(counts * hot0, axis=1, keepdims=True) + base
        slot1 = jnp.sum(counts * hot1, axis=1, keepdims=True) + base
        col = lax.broadcasted_iota(jnp.int32, (Q_DEV, RCV), 1)
        slot = (col % ROWS).astype(F32)
        which = (col // (2 * ROWS)).astype(F32)
        mix = jnp.where((slot == slot0) & (which == first), weight0, 0.0) + jnp.where(
            (slot == slot1) & (which == second), weight1, 0.0
        )
        for part, value in enumerate(three_parts(mix)):
            mix_ref[part * Q_DEV : (part + 1) * Q_DEV, :] = value.astype(BF16)

    total = stream_ref[...].astype(F32)
    for z in range(NZ):
        moved = dot_nn(mix_ref[...], returned_ref[z])
        total = total + moved[:Q_DEV] + moved[Q_DEV : 2 * Q_DEV] + moved[2 * Q_DEV :]
    out_ref[...] = total.astype(BF16)


def combine(returned, stream, routes):
    return pl.pallas_call(
        combine_kernel,
        grid=(SLICE // C_BLOCK,),
        out_shape=jax.ShapeDtypeStruct((Q_DEV, SLICE), BF16),
        in_specs=[
            pl.BlockSpec((NZ, RCV, C_BLOCK), lambda i: (0, 0, i)),
            pl.BlockSpec((Q_DEV, C_BLOCK), lambda i: (0, i)),
            pl.BlockSpec(routes.shape, lambda i: (0, 0)),
        ],
        out_specs=pl.BlockSpec((Q_DEV, C_BLOCK), lambda i: (0, i)),
        scratch_shapes=[pltpu.VMEM((3 * Q_DEV, RCV), BF16)],
        compiler_params=params(40),
        cost_estimate=pl.CostEstimate(flops=7 * 10**8, bytes_accessed=4 * 10**6, transcendentals=0),
        name="combine",
    )(returned, stream, routes)


def body(
    residual,
    queries,
    new_keys,
    new_values,
    cache_keys,
    cache_values,
    out_weight,
    norm_gain,
    route_ids,
    route_weight,
    gate_weight,
    up_weight,
    down_weight,
):
    core = lax.axis_index("c")
    mine = lax.axis_index(XY) * 2 + core
    depth = lax.axis_index("z")

    far_keys = other_core(cache_keys)
    far_values = other_core(cache_values)
    far_new = other_core(jnp.concatenate([new_keys, new_values], axis=1))
    head_width = HEADS * HD
    weight_t = lax.all_gather(out_weight.T, XY + ("c",), axis=0, tiled=True)
    all_queries = exchange(
        jnp.broadcast_to(queries[None], (PLANE, Q_DEV, head_width)), XY
    ).reshape(PLANE * Q_DEV, head_width)
    place = jnp.stack([core, mine]).astype(jnp.int32)
    partial = attend(
        place, all_queries, cache_keys, far_keys, new_keys, far_new[:, :head_width],
        cache_values, far_values, new_values, far_new[:, head_width:],
    )
    far_gate = other_core(gate_weight)
    far_up = other_core(up_weight)
    far_down = other_core(down_weight)

    tok = residual.shape[0]
    codes = jnp.concatenate(
        [
            route_ids.astype(F32),
            jnp.stack(three_parts(route_weight[:, 0]) + three_parts(route_weight[:, 1]), axis=1),
        ],
        axis=1,
    ).astype(BF16)
    codes = jnp.pad(codes, ((0, 0), (0, PACK - codes.shape[1])))
    own = jnp.transpose(residual.reshape(tok, NZ, SLICE), (1, 0, 2))
    own = jnp.concatenate([own, jnp.broadcast_to(codes[None], (NZ, tok, PACK))], axis=2)
    own = exchange(own, ("z",)).reshape(Q_DEV, SLICE + PACK)
    routes = own[:, SLICE:].astype(F32)
    routes_t = routes[:, :8].T

    parts = exchange(partial.reshape(PLANE, Q_DEV, WIDE), XY)
    heads = exchange(project(parts, weight_t), ("z",))
    gain = lax.dynamic_slice_in_dim(norm_gain, depth * SLICE, SLICE, 0)[None]
    stream, packed = pack(heads, own[:, :SLICE], gain, routes_t)
    copies = jnp.broadcast_to(
        packed.reshape(1, E, 1, ROWS, SLICE), (NZ, E, 2, ROWS, SLICE)
    ).reshape(NZ * PLANE, ROWS, SLICE)
    arrived = exchange(copies, ZXY).reshape(NZ, RCV, SLICE)
    hidden = hidden_units(arrived, gate_weight, far_gate, up_weight, far_up)
    answers = down_units(hidden, down_weight, far_down)
    returned = exchange(answers.reshape(NZ * PLANE, ROWS, SLICE), ZXY).reshape(NZ, RCV, SLICE)
    layer = combine(returned, stream, routes)
    final = exchange(layer.reshape(NZ, tok, SLICE), ("z",))
    return jnp.transpose(final, (1, 0, 2)).reshape(tok, D)


def solution(mesh):
    split = Mesh(mesh.devices.reshape(4, 2, 2, 2, NZ), ("y", "xh", "xl", "c", "z"))
    dp = ("y", "xh", "xl", "c")
    rows = dp + ("z",)
    placed = (
        P(rows, None),
        P(dp, "z"),
        P(dp, "z"),
        P(dp, "z"),
        P(dp, "z"),
        P(dp, "z"),
        P("z", dp),
        P(),
        P(rows, None),
        P(rows, None),
        P(None, rows),
        P(None, rows),
        P(rows, None),
    )
    return jax.shard_map(body, mesh=split, in_specs=placed, out_specs=P(rows, None), check_vma=False)
```

```python
import functools
import math

import jax
import jax.numpy as jnp
from jax import lax
from jax.experimental import pallas as pl
from jax.experimental.pallas import tpu as pltpu
from jax.sharding import Mesh, PartitionSpec as P

D = 4608
HD = 128
HEADS = 5
E = 8
TOP = 2
CAP = 5
NZ = 4
PLANE = 16
Q_DEV = 64
SLICE = D // NZ
MAIN = 16
OVER = NZ * CAP - MAIN
THIRD = SLICE // 3
CHUNK = SLICE + THIRD
PACK = 128
WIDE = HEADS * HD + PACK
NORM_EPS = 1e-06
NEGATIVE = -1e30
TO_BASE2 = math.log2(math.e) / math.sqrt(HD)

XY = ("y", "xh", "xl")
ZXY = ("z", "y", "xh", "xl")
F32 = jnp.float32
BF16 = jnp.bfloat16


VMEM = pl.BlockSpec(memory_space=pltpu.VMEM)
HBM = pl.BlockSpec(memory_space=pltpu.HBM)


def params(mib):
    return pltpu.CompilerParams(vmem_limit_bytes=mib * 2**20)


def exchange(block, axes):
    return lax.all_to_all(block, axes, split_axis=0, concat_axis=0, tiled=True)


def other_core(block):
    return lax.ppermute(block, "c", [(0, 1), (1, 0)])


def around_z(blocks, depth):
    take = lambda a, i: lax.dynamic_index_in_dim(a, i % NZ, 0, keepdims=False)
    got = [take(blocks, depth)]
    for step in range(1, NZ):
        route = [(i, (i + step) % NZ) for i in range(NZ)]
        got.append(lax.ppermute(take(blocks, depth + step), "z", route))
    got = jnp.stack(got)
    return jnp.stack([take(got, depth - i + NZ) for i in range(NZ)])


def three_parts(value):
    high = value.astype(BF16).astype(F32)
    rest = value - high
    middle = rest.astype(BF16).astype(F32)
    return high, middle, (rest - middle).astype(BF16).astype(F32)


def dot_nt(a, b, **kw):
    return lax.dot_general(a, b, (((1,), (1,)), ((), ())), preferred_element_type=F32, **kw)


def dot_nn(a, b, **kw):
    return lax.dot_general(a, b, (((1,), (0,)), ((), ())), preferred_element_type=F32, **kw)


Q_BLOCKS = 8


def attend_kernel(place_ref, q_ref, ka_ref, kb_ref, na_ref, nb_ref, va_ref, vb_ref, wa_ref, wb_ref, out_ref):
    core, mine = place_ref[0], place_ref[1]
    rows = out_ref.shape[0]
    row = lax.broadcasted_iota(jnp.int32, (rows, HD), 0)
    lane = lax.broadcasted_iota(jnp.int32, (rows, HD), 1)
    block = pl.program_id(0) * Q_BLOCKS + row // Q_DEV
    q_pos = (block * 2 + core) * Q_DEV + row % Q_DEV
    k_pos = jnp.where(lane < Q_DEV, mine * Q_DEV + lane, (mine + 1 - 2 * core) * Q_DEV + lane - Q_DEV)
    allowed = k_pos <= q_pos
    pack = jnp.zeros((rows, PACK), F32)
    for h in range(HEADS):
        cols = slice(h * HD, (h + 1) * HD)
        q = q_ref[:, :, cols].reshape(rows, HD)
        s1 = dot_nt(q, ka_ref[:, cols])
        s2 = dot_nt(q, kb_ref[:, cols])
        fresh = jnp.concatenate([na_ref[:, cols], nb_ref[:, cols]], axis=0)
        s3 = jnp.where(allowed, dot_nt(q, fresh), NEGATIVE)
        top = jnp.maximum(
            jnp.maximum(jnp.max(s1, axis=1, keepdims=True), jnp.max(s2, axis=1, keepdims=True)),
            jnp.max(s3, axis=1, keepdims=True),
        ) * TO_BASE2
        w1 = jnp.exp2(s1 * TO_BASE2 - top)
        w2 = jnp.exp2(s2 * TO_BASE2 - top)
        w3 = jnp.exp2(s3 * TO_BASE2 - top)
        total = (
            jnp.sum(w1, axis=1, keepdims=True)
            + jnp.sum(w2, axis=1, keepdims=True)
            + jnp.sum(w3, axis=1, keepdims=True)
        )
        fresh_v = jnp.concatenate([wa_ref[:, cols], wb_ref[:, cols]], axis=0)
        acc = (
            dot_nn(w1.astype(BF16), va_ref[:, cols])
            + dot_nn(w2.astype(BF16), vb_ref[:, cols])
            + dot_nn(w3.astype(BF16), fresh_v)
        )
        out_ref[:, cols] = (acc / total).astype(BF16)
        for part, value in enumerate(three_parts(top + jnp.log2(total))):
            pack = jnp.where(lane == part * 8 + h, value, pack)
    out_ref[:, HEADS * HD :] = pack.astype(BF16)


def attend(place, q, *keys):
    rows = Q_BLOCKS * Q_DEV
    whole = [pl.BlockSpec(a.shape, lambda i: (0, 0)) for a in keys]
    return pl.pallas_call(
        attend_kernel,
        grid=(PLANE // Q_BLOCKS,),
        out_shape=jax.ShapeDtypeStruct((PLANE * Q_DEV, WIDE), BF16),
        in_specs=[
            pl.BlockSpec(memory_space=pltpu.SMEM),
            pl.BlockSpec((Q_BLOCKS, Q_DEV, HEADS * HD), lambda i: (i, 0, 0)),
            *whole,
        ],
        out_specs=pl.BlockSpec((rows, WIDE), lambda i: (i, 0)),
        compiler_params=params(56),
        cost_estimate=pl.CostEstimate(flops=11 * 10**9, bytes_accessed=10**7, transcendentals=11 * 10**6),
        name="attend",
    )(place, q, *keys)


def merge(parts_ref, out_ref):
    count = parts_ref.shape[0]
    sums = [parts_ref[i, :, HEADS * HD :].astype(F32) for i in range(count)]
    for h in range(HEADS):
        cols = slice(h * HD, (h + 1) * HD)
        logs = [s[:, h : h + 1] + s[:, 8 + h : 9 + h] + s[:, 16 + h : 17 + h] for s in sums]
        top = functools.reduce(jnp.maximum, logs)
        shares = [jnp.exp2(v - top) for v in logs]
        total = functools.reduce(jnp.add, shares)
        acc = functools.reduce(
            jnp.add, [shares[i] * parts_ref[i, :, cols].astype(F32) for i in range(count)]
        )
        out_ref[:, cols] = (acc / total).astype(BF16)


def project_kernel(parts_ref, weight_ref, out_ref, attended_ref):
    @pl.when(pl.program_id(0) == 0)
    def _():
        merge(parts_ref, attended_ref)

    out_ref[0] = dot_nt(attended_ref[...], weight_ref[...]).astype(BF16)


def project(parts, weight):
    width = HEADS * HD
    return pl.pallas_call(
        project_kernel,
        grid=(NZ,),
        out_shape=jax.ShapeDtypeStruct((NZ, Q_DEV, SLICE), BF16),
        in_specs=[
            pl.BlockSpec(parts.shape, lambda i: (0, 0, 0)),
            pl.BlockSpec((SLICE, width), lambda i: (i, 0)),
        ],
        out_specs=pl.BlockSpec((1, Q_DEV, SLICE), lambda i: (i, 0, 0)),
        scratch_shapes=[pltpu.VMEM((Q_DEV, width), BF16)],
        compiler_params=params(58),
        cost_estimate=pl.CostEstimate(flops=4 * 10**8, bytes_accessed=8 * 10**6, transcendentals=0),
        name="project",
    )(parts, weight)


def earlier():
    i = lax.broadcasted_iota(jnp.int32, (Q_DEV, Q_DEV), 0)
    j = lax.broadcasted_iota(jnp.int32, (Q_DEV, Q_DEV), 1)
    return i, j


def pack_kernel(heads_ref, own_ref, gain_ref, stream_ref, routes_ref, chunk_ref, made_ref, sems):
    total = own_ref[:, :SLICE].astype(F32)
    summed = heads_ref[0].astype(F32)
    for z in range(1, NZ):
        summed = summed + heads_ref[z].astype(F32)
    stream = (total + summed).astype(BF16)
    stream_ref[...] = stream
    stream_f = stream.astype(F32)
    squares = stream_f * stream_f
    scaled = (stream_f * gain_ref[...]).astype(BF16)
    routes = own_ref[:, SLICE:]
    routes_ref[...] = routes.astype(F32)
    kind, lane = iotas(8, PACK)
    turned = dot_nt(jnp.where(kind == lane, 1.0, 0.0).astype(BF16), routes)
    first, second = turned[0:1, :], turned[1:2, :]
    expert = lax.broadcasted_iota(jnp.int32, (E, Q_DEV), 0).astype(F32)
    hot0 = jnp.where(expert == first, 1.0, 0.0)
    hot1 = jnp.where(expert == second, 1.0, 0.0)
    j, i = earlier()
    before_t = jnp.where((j < i) & (j // 16 == i // 16), 1.0, 0.0)
    counts = dot_nn((hot0 + hot1).astype(BF16), before_t.astype(BF16))
    base = (lax.broadcasted_iota(jnp.int32, (1, Q_DEV), 1) // 16 * CAP).astype(F32)
    slot0 = jnp.sum(counts * hot0, axis=0, keepdims=True) + base
    slot1 = jnp.sum(counts * hot1, axis=0, keepdims=True) + base

    def placing(slot, which):
        return jnp.where(
            ((slot == slot0) & (which == first)) | ((slot == slot1) & (which == second)), 1.0, 0.0
        )

    line = lax.broadcasted_iota(jnp.int32, (E * MAIN, Q_DEV), 0)
    which = (line // MAIN).astype(F32)
    part = line % MAIN
    main = dot_nn(placing(part.astype(F32), which).astype(BF16), scaled).astype(BF16)
    over = jnp.zeros((E * MAIN, THIRD), F32)
    for t in range(3):
        wanted = jnp.where(part // OVER == t, MAIN + part % OVER, -1).astype(F32)
        over = over + dot_nn(placing(wanted, which).astype(BF16), scaled[:, t * THIRD : (t + 1) * THIRD])
    sums_row = dot_nt(jnp.ones((8, SLICE), F32), squares, precision=lax.Precision.HIGHEST)
    slot = lax.broadcasted_iota(jnp.int32, (HD, Q_DEV), 0).astype(F32)
    row = lax.broadcasted_iota(jnp.int32, (MAIN, HD), 0)
    for e in range(E):
        placed = dot_nt(sums_row, placing(slot, float(e)), precision=lax.Precision.HIGHEST)[0:1, :]
        high, middle, low = three_parts(placed)
        extra = jnp.where(
            row == 3 * OVER,
            high,
            jnp.where(row == 3 * OVER + 1, middle, jnp.where(row == 3 * OVER + 2, low, 0.0)),
        )
        here = slice(e * MAIN, (e + 1) * MAIN)
        begin = (over[here, :HD] + extra).astype(BF16)
        rest = over[here, HD:].astype(BF16)
        made_ref[e, :, :SLICE] = main[here]
        made_ref[e, :, SLICE : SLICE + HD] = begin
        made_ref[e, :, SLICE + HD :] = rest
    copies = [
        pltpu.make_async_copy(made_ref, chunk_ref.at[z, :, x], sems.at[z, x])
        for z in range(NZ)
        for x in range(2)
    ]
    for copy in copies:
        copy.start()
    for copy in copies:
        copy.wait()


def pack(heads, own, gain):
    return pl.pallas_call(
        pack_kernel,
        out_shape=(
            jax.ShapeDtypeStruct((Q_DEV, SLICE), BF16),
            jax.ShapeDtypeStruct((Q_DEV, PACK), F32),
            jax.ShapeDtypeStruct((NZ, E, 2, MAIN, CHUNK), BF16),
        ),
        in_specs=[VMEM] * 3,
        out_specs=(VMEM, VMEM, HBM),
        scratch_shapes=[pltpu.VMEM((E, MAIN, CHUNK), BF16), pltpu.SemaphoreType.DMA((NZ, 2))],
        compiler_params=params(40),
        cost_estimate=pl.CostEstimate(flops=3 * 10**7, bytes_accessed=5 * 10**6, transcendentals=0),
        name="pack",
    )(heads, own, gain)


RCV = PLANE * MAIN
F_BLOCK = 256
EXT = PLANE * OVER
ALL = RCV + EXT
def iotas(rows, cols):
    return (
        lax.broadcasted_iota(jnp.int32, (rows, cols), 0),
        lax.broadcasted_iota(jnp.int32, (rows, cols), 1),
    )


def unpack(x_ref, rows_ref):
    over_row, line = iotas(EXT, RCV)
    extra_sum = jnp.zeros((RCV, HD), F32)
    for z in range(NZ):
        rows_ref[:RCV, z * SLICE : (z + 1) * SLICE] = x_ref[z, :, :SLICE]
        over = x_ref[z, :, SLICE:]
        extra_sum = extra_sum + over[:, :HD].astype(F32)
        for t in range(3):
            pick = (line // MAIN == over_row // OVER) & (line % MAIN == t * OVER + over_row % OVER)
            rows_ref[RCV:, z * SLICE + t * THIRD : z * SLICE + (t + 1) * THIRD] = dot_nn(
                jnp.where(pick, 1.0, 0.0).astype(BF16), over
            ).astype(BF16)

    source, line = iotas(PLANE, RCV)
    part = line % MAIN
    pick = (line // MAIN == source) & (part >= 3 * OVER) & (part < 3 * OVER + 3)
    sums = dot_nn(jnp.where(pick, 1.0, 0.0), extra_sum, precision=lax.Precision.HIGHEST)
    row, source = iotas(ALL, PLANE)
    owner = jnp.where(row < RCV, row // MAIN, (row - RCV) // OVER)
    spread = dot_nn(jnp.where(owner == source, 1.0, 0.0), sums, precision=lax.Precision.HIGHEST)
    row, lane = iotas(ALL, HD)
    slot = jnp.where(row < RCV, row % MAIN, MAIN + (row - RCV) % OVER)
    column = jnp.sum(jnp.where(lane == slot, spread, 0.0), axis=1, keepdims=True)
    return lax.rsqrt(column * (1.0 / D) + NORM_EPS)


def repack(answer, made_ref, z):
    width = answer.shape[1]
    made_ref[z, :, :width] = answer[:RCV]
    line, over_row = iotas(RCV, EXT)
    for third in range(width // THIRD):
        over = jnp.zeros((RCV, HD), F32)
        for t in range(3):
            pick = (line // MAIN == over_row // OVER) & (line % MAIN == t * OVER + over_row % OVER)
            at = third * THIRD + t * HD
            over = over + dot_nn(jnp.where(pick, 1.0, 0.0).astype(BF16), answer[RCV:, at : at + HD])
        made_ref[z, :, width + third * HD : width + (third + 1) * HD] = over.astype(BF16)


AHEAD = 2
SLOTS = AHEAD + 1


def experts_kernel(
    x_ref, ga_hbm, gb_hbm, ua_hbm, ub_hbm, da_hbm, db_hbm, out_hbm,
    made_ref, rows_ref, scale_ref, hidden_ref, gate_ref, up_ref, down_ref, weight_sem, down_sem, out_sem,
):
    steps = ga_hbm.shape[1] // F_BLOCK

    def weight_copies(step, gate_hbm, up_hbm, block):
        cols = pl.ds(pl.multiple_of(block * F_BLOCK, F_BLOCK), F_BLOCK)
        slot = lax.rem(step, SLOTS)
        return (
            pltpu.make_async_copy(gate_hbm.at[:, cols], gate_ref.at[slot], weight_sem.at[0, slot]),
            pltpu.make_async_copy(up_hbm.at[:, cols], up_ref.at[slot], weight_sem.at[1, slot]),
        )

    def down_copies():
        return [
            [
                pltpu.make_async_copy(
                    hbm.at[:, z * SLICE : (z + 1) * SLICE], down_ref.at[side, z], down_sem.at[side, z]
                )
                for side, hbm in enumerate((da_hbm, db_hbm))
            ]
            for z in range(NZ)
        ]

    for step in range(AHEAD):
        for copy in weight_copies(step, ga_hbm, ua_hbm, step):
            copy.start()
    scale_ref[...] = jnp.broadcast_to(unpack(x_ref, rows_ref), (ALL, HD))

    @pl.loop(0, 2 * steps)
    def _(step):
        later = step + AHEAD

        @pl.when(later < steps)
        def _():
            for copy in weight_copies(later, ga_hbm, ua_hbm, later):
                copy.start()

        @pl.when((later >= steps) & (later < 2 * steps))
        def _():
            for copy in weight_copies(later, gb_hbm, ub_hbm, later - steps):
                copy.start()

        @pl.when(later == 2 * steps)
        def _():
            for pair in down_copies():
                for copy in pair:
                    copy.start()

        for copy in weight_copies(step, ga_hbm, ua_hbm, 0):
            copy.wait()
        slot = lax.rem(step, SLOTS)
        gate = dot_nn(rows_ref[...], gate_ref[slot]) * scale_ref[:, :1]
        up = dot_nn(rows_ref[...], up_ref[slot]) * scale_ref[:, :1]
        to = pl.ds(pl.multiple_of(step * F_BLOCK, F_BLOCK), F_BLOCK)
        hidden_ref[:, to] = (gate / (1.0 + jnp.exp(-gate)) * up).astype(BF16)

    half = da_hbm.shape[0]
    sent = []
    for z, pair in enumerate(down_copies()):
        for copy in pair:
            copy.wait()
        answer = dot_nn(hidden_ref[:, :half], down_ref[0, z]) + dot_nn(hidden_ref[:, half:], down_ref[1, z])
        repack(answer.astype(BF16), made_ref, z)
        sent.append(pltpu.make_async_copy(made_ref.at[z], out_hbm.at[z], out_sem.at[z]))
        sent[-1].start()
    for copy in sent:
        copy.wait()


def experts(x, ga, gb, ua, ub, da, db):
    width = ga.shape[1]
    return pl.pallas_call(
        experts_kernel,
        out_shape=jax.ShapeDtypeStruct(x.shape, BF16),
        in_specs=[VMEM] + [HBM] * 6,
        out_specs=HBM,
        scratch_shapes=[
            pltpu.VMEM(x.shape, BF16),
            pltpu.VMEM((ALL, D), BF16),
            pltpu.VMEM((ALL, HD), F32),
            pltpu.VMEM((ALL, 2 * width), BF16),
            pltpu.VMEM((SLOTS, D, F_BLOCK), BF16),
            pltpu.VMEM((SLOTS, D, F_BLOCK), BF16),
            pltpu.VMEM((2, NZ, width, SLICE), BF16),
            pltpu.SemaphoreType.DMA((2, SLOTS)),
            pltpu.SemaphoreType.DMA((2, NZ)),
            pltpu.SemaphoreType.DMA((NZ,)),
        ],
        compiler_params=params(56),
        cost_estimate=pl.CostEstimate(flops=14 * 10**9, bytes_accessed=48 * 10**6, transcendentals=10**6),
        name="experts",
    )(x, ga, gb, ua, ub, da, db)


def mixing_kernel(routes_ref, mix_ref):
    first, second = routes_ref[:, 0:1], routes_ref[:, 1:2]
    weight0 = routes_ref[:, 2:3] + routes_ref[:, 3:4] + routes_ref[:, 4:5]
    weight1 = routes_ref[:, 5:6] + routes_ref[:, 6:7] + routes_ref[:, 7:8]
    expert = lax.broadcasted_iota(jnp.int32, (Q_DEV, HD), 1).astype(F32)
    hot0 = jnp.where(expert == first, 1.0, 0.0)
    hot1 = jnp.where(expert == second, 1.0, 0.0)
    i, j = earlier()
    before = jnp.where((j < i) & (j // 16 == i // 16), 1.0, 0.0)
    counts = dot_nn(before.astype(BF16), (hot0 + hot1).astype(BF16))
    base = (lax.broadcasted_iota(jnp.int32, (Q_DEV, 1), 0) // 16 * CAP).astype(F32)
    slot0 = jnp.sum(counts * hot0, axis=1, keepdims=True) + base
    slot1 = jnp.sum(counts * hot1, axis=1, keepdims=True) + base
    col = lax.broadcasted_iota(jnp.int32, (Q_DEV, RCV), 1)
    part = col % MAIN
    which = (col // (2 * MAIN)).astype(F32)
    for kind in range(4):
        slot = part if kind == 0 else jnp.where(part // OVER == kind - 1, MAIN + part % OVER, -1)
        slot = slot.astype(F32)
        mix = jnp.where((slot == slot0) & (which == first), weight0, 0.0) + jnp.where(
            (slot == slot1) & (which == second), weight1, 0.0
        )
        for at, value in enumerate(three_parts(mix)):
            mix_ref[kind, at * Q_DEV : (at + 1) * Q_DEV, :] = value.astype(BF16)


def mixing(routes):
    return pl.pallas_call(
        mixing_kernel,
        out_shape=jax.ShapeDtypeStruct((4, 3 * Q_DEV, RCV), BF16),
        compiler_params=params(30),
        cost_estimate=pl.CostEstimate(flops=10**6, bytes_accessed=4 * 10**5, transcendentals=0),
        name="mixing",
    )(routes)


def combine_kernel(returned_hbm, stream_ref, mix_ref, out_ref, returned_ref, sems):
    copies = [
        pltpu.make_async_copy(returned_hbm.at[z], returned_ref.at[z], sems.at[z]) for z in range(NZ)
    ]
    for copy in copies:
        copy.start()

    def fold(kind, block):
        moved = dot_nn(mix_ref[kind], block)
        return moved[:Q_DEV] + moved[Q_DEV : 2 * Q_DEV] + moved[2 * Q_DEV :]

    total = stream_ref[...].astype(F32)
    extra = [jnp.zeros((Q_DEV, HD), F32)] * (SLICE // HD)
    for z in range(NZ):
        copies[z].wait()
        total = total + fold(0, returned_ref[z, :, :SLICE])
        for at in range(SLICE // HD):
            lanes = slice(SLICE + at // 3 * HD, SLICE + (at // 3 + 1) * HD)
            extra[at] = extra[at] + fold(at % 3 + 1, returned_ref[z, :, lanes])
    for at, part in enumerate(extra):
        cols = slice(at * HD, (at + 1) * HD)
        out_ref[:, cols] = (total[:, cols] + part).astype(BF16)


def combine(returned, stream, mix):
    return pl.pallas_call(
        combine_kernel,
        out_shape=jax.ShapeDtypeStruct((Q_DEV, SLICE), BF16),
        in_specs=[HBM, VMEM, VMEM],
        out_specs=VMEM,
        scratch_shapes=[pltpu.VMEM(returned.shape, BF16), pltpu.SemaphoreType.DMA((NZ,))],
        compiler_params=params(40),
        cost_estimate=pl.CostEstimate(flops=7 * 10**8, bytes_accessed=5 * 10**6, transcendentals=0),
        name="combine",
    )(returned, stream, mix)


def body(
    residual,
    queries,
    new_keys,
    new_values,
    cache_keys,
    cache_values,
    out_weight,
    norm_gain,
    route_ids,
    route_weight,
    gate_weight,
    up_weight,
    down_weight,
):
    core = lax.axis_index("c")
    mine = lax.axis_index(XY) * 2 + core
    depth = lax.axis_index("z")

    head_width = HEADS * HD
    far_keys = other_core(cache_keys)
    far_values = other_core(cache_values)
    far_new_keys = other_core(new_keys)
    far_new_values = other_core(new_values)
    weight_t = lax.all_gather(out_weight.T, XY + ("c",), axis=0, tiled=True)
    all_queries = exchange(jnp.broadcast_to(queries[None], (PLANE, Q_DEV, head_width)), XY)
    tok = residual.shape[0]
    codes = jnp.concatenate(
        [
            route_ids.astype(F32),
            jnp.stack(three_parts(route_weight[:, 0]) + three_parts(route_weight[:, 1]), axis=1),
        ],
        axis=1,
    ).astype(BF16)
    codes = jnp.pad(codes, ((0, 0), (0, PACK - codes.shape[1])))
    own = jnp.transpose(residual.reshape(tok, NZ, SLICE), (1, 0, 2))
    own = jnp.concatenate([own, jnp.broadcast_to(codes[None], (NZ, tok, PACK))], axis=2)
    own = around_z(own, depth).reshape(Q_DEV, SLICE + PACK)
    own, all_queries = lax.optimization_barrier((own, all_queries))

    place = jnp.stack([core, mine]).astype(jnp.int32)
    partial = attend(
        place, all_queries, cache_keys, far_keys, new_keys, far_new_keys,
        cache_values, far_values, new_values, far_new_values,
    )
    after = lax.optimization_barrier((gate_weight, up_weight, down_weight, all_queries))
    far_gate, far_up, far_down = (other_core(w) for w in after[:3])
    parts = exchange(partial.reshape(PLANE, Q_DEV, WIDE), XY)
    heads = exchange(project(parts, weight_t), ("z",))
    gain = lax.dynamic_slice_in_dim(norm_gain, depth * SLICE, SLICE, 0)[None]
    stream, routes, chunks = pack(heads, own, gain)
    mix = mixing(routes)
    arrived = exchange(chunks.reshape(NZ * PLANE, MAIN, CHUNK), ZXY).reshape(NZ, RCV, CHUNK)
    answers = experts(arrived, gate_weight, far_gate, up_weight, far_up, down_weight, far_down)
    returned = exchange(answers.reshape(NZ * PLANE, MAIN, CHUNK), ZXY).reshape(NZ, RCV, CHUNK)
    layer = combine(returned, stream, mix)
    final = exchange(layer.reshape(NZ, tok, SLICE), ("z",))
    return jnp.transpose(final, (1, 0, 2)).reshape(tok, D)


def solution(mesh):
    split = Mesh(mesh.devices.reshape(4, 2, 2, 2, NZ), ("y", "xh", "xl", "c", "z"))
    dp = ("y", "xh", "xl", "c")
    rows = dp + ("z",)
    placed = (
        P(rows, None),
        P(dp, "z"),
        P(dp, "z"),
        P(dp, "z"),
        P(dp, "z"),
        P(dp, "z"),
        P("z", dp),
        P(),
        P(rows, None),
        P(rows, None),
        P(None, rows),
        P(None, rows),
        P(rows, None),
    )
    return jax.shard_map(body, mesh=split, in_specs=placed, out_specs=P(rows, None), check_vma=False)
```

```python
import functools
import math

import jax
import jax.numpy as jnp
from jax import lax
from jax.experimental import pallas as pl
from jax.experimental.pallas import tpu as pltpu
from jax.sharding import Mesh, PartitionSpec as P

D = 4608
HD = 128
HEADS = 5
E = 8
TOP = 2
CAP = 5
NZ = 4
PLANE = 16
Q_DEV = 64
SLICE = D // NZ
MAIN = 16
OVER = NZ * CAP - MAIN
THIRD = SLICE // 3
CHUNK = SLICE + THIRD
PACK = 128
LINES = HEADS * Q_DEV + 8
NORM_EPS = 1e-06
NEGATIVE = -1e30
TO_BASE2 = math.log2(math.e) / math.sqrt(HD)

XY = ("y", "xh", "xl")
ZXY = ("z", "y", "xh", "xl")
F32 = jnp.float32
BF16 = jnp.bfloat16


VMEM = pl.BlockSpec(memory_space=pltpu.VMEM)
HBM = pl.BlockSpec(memory_space=pltpu.HBM)
ANY = pl.BlockSpec(memory_space=pl.ANY)


def params(mib):
    return pltpu.CompilerParams(vmem_limit_bytes=mib * 2**20)


def exchange(block, axes):
    return lax.all_to_all(block, axes, split_axis=0, concat_axis=0, tiled=True)


def other_core(block):
    return lax.ppermute(block, "c", [(0, 1), (1, 0)])


def around_z(blocks, depth):
    take = lambda a, i: lax.dynamic_index_in_dim(a, i % NZ, 0, keepdims=False)
    got = [take(blocks, depth)]
    for step in range(1, NZ):
        route = [(i, (i + step) % NZ) for i in range(NZ)]
        got.append(lax.ppermute(take(blocks, depth + step), "z", route))
    got = jnp.stack(got)
    return jnp.stack([take(got, depth - i + NZ) for i in range(NZ)])


def three_parts(value):
    high = value.astype(BF16).astype(F32)
    rest = value - high
    middle = rest.astype(BF16).astype(F32)
    return high, middle, (rest - middle).astype(BF16).astype(F32)


def dot_nt(a, b, **kw):
    return lax.dot_general(a, b, (((1,), (1,)), ((), ())), preferred_element_type=F32, **kw)


def dot_nn(a, b, **kw):
    return lax.dot_general(a, b, (((1,), (0,)), ((), ())), preferred_element_type=F32, **kw)


Q_BLOCKS = 8


def attend_kernel(place_ref, q_ref, ka_ref, kb_ref, na_ref, nb_ref, va_ref, vb_ref, wa_ref, wb_ref, out_ref):
    core, mine = place_ref[0], place_ref[1]
    rows = Q_BLOCKS * Q_DEV
    row = lax.broadcasted_iota(jnp.int32, (rows, HD), 0)
    lane = lax.broadcasted_iota(jnp.int32, (rows, HD), 1)
    block = pl.program_id(0) * Q_BLOCKS + row // Q_DEV
    q_pos = (block * 2 + core) * Q_DEV + row % Q_DEV
    k_pos = jnp.where(lane < Q_DEV, mine * Q_DEV + lane, (mine + 1 - 2 * core) * Q_DEV + lane - Q_DEV)
    allowed = k_pos <= q_pos
    pack = jnp.zeros((rows, PACK), F32)
    group = row % Q_DEV // 8 * 16
    for h in range(HEADS):
        cols = slice(h * HD, (h + 1) * HD)
        q = q_ref[:, :, cols].reshape(rows, HD)
        s1 = dot_nt(q, ka_ref[:, cols])
        s2 = dot_nt(q, kb_ref[:, cols])
        fresh = jnp.concatenate([na_ref[:, cols], nb_ref[:, cols]], axis=0)
        s3 = jnp.where(allowed, dot_nt(q, fresh), NEGATIVE)
        top = jnp.maximum(
            jnp.maximum(jnp.max(s1, axis=1, keepdims=True), jnp.max(s2, axis=1, keepdims=True)),
            jnp.max(s3, axis=1, keepdims=True),
        ) * TO_BASE2
        w1 = jnp.exp2(s1 * TO_BASE2 - top)
        w2 = jnp.exp2(s2 * TO_BASE2 - top)
        w3 = jnp.exp2(s3 * TO_BASE2 - top)
        total = (
            jnp.sum(w1, axis=1, keepdims=True)
            + jnp.sum(w2, axis=1, keepdims=True)
            + jnp.sum(w3, axis=1, keepdims=True)
        )
        fresh_v = jnp.concatenate([wa_ref[:, cols], wb_ref[:, cols]], axis=0)
        acc = (
            dot_nn(w1.astype(BF16), va_ref[:, cols])
            + dot_nn(w2.astype(BF16), vb_ref[:, cols])
            + dot_nn(w3.astype(BF16), fresh_v)
        )
        out_ref[:, h * Q_DEV : (h + 1) * Q_DEV, :] = (
            (acc / total).astype(BF16).reshape(Q_BLOCKS, Q_DEV, HD)
        )
        for part, value in enumerate(three_parts(top + jnp.log2(total))):
            pack = jnp.where(lane == group + part * HEADS + h, value, pack)
    folded = jnp.sum(pack.reshape(Q_BLOCKS, 8, 8, PACK), axis=1)
    out_ref[:, HEADS * Q_DEV :, :] = folded.astype(BF16)


def attend(place, q, *keys):
    whole = [pl.BlockSpec(a.shape, lambda i: (0, 0)) for a in keys]
    return pl.pallas_call(
        attend_kernel,
        grid=(PLANE // Q_BLOCKS,),
        out_shape=jax.ShapeDtypeStruct((PLANE, LINES, HD), BF16),
        in_specs=[
            pl.BlockSpec(memory_space=pltpu.SMEM),
            pl.BlockSpec((Q_BLOCKS, Q_DEV, HEADS * HD), lambda i: (i, 0, 0)),
            *whole,
        ],
        out_specs=pl.BlockSpec((Q_BLOCKS, LINES, HD), lambda i: (i, 0, 0)),
        compiler_params=params(56),
        cost_estimate=pl.CostEstimate(flops=11 * 10**9, bytes_accessed=10**7, transcendentals=11 * 10**6),
        name="attend",
    )(place, q, *keys)


def merge(parts_ref, out_ref):
    count = parts_ref.shape[0]
    sums = [parts_ref[i, HEADS * Q_DEV :, :].astype(F32) for i in range(count)]
    sums = [
        s + pltpu.roll(s, PACK - HEADS, axis=1) + pltpu.roll(s, PACK - 2 * HEADS, axis=1) for s in sums
    ]
    for h in range(HEADS):
        logs = [
            jnp.concatenate([s[:, g * 16 + h : g * 16 + h + 1] for g in range(8)], axis=0) for s in sums
        ]
        top = functools.reduce(jnp.maximum, logs)
        shares = [jnp.exp2(v - top) for v in logs]
        total = functools.reduce(jnp.add, shares)
        acc = functools.reduce(
            jnp.add,
            [
                shares[i] * parts_ref[i, h * Q_DEV : (h + 1) * Q_DEV, :].astype(F32)
                for i in range(count)
            ],
        )
        out_ref[:, h * HD : (h + 1) * HD] = (acc / total).astype(BF16)


def project_kernel(parts_ref, weight_ref, out_ref, attended_ref):
    @pl.when(pl.program_id(0) == 0)
    def _():
        merge(parts_ref, attended_ref)

    out_ref[0] = dot_nt(attended_ref[...], weight_ref[...]).astype(BF16)


def project(parts, weight):
    width = HEADS * HD
    return pl.pallas_call(
        project_kernel,
        grid=(NZ,),
        out_shape=jax.ShapeDtypeStruct((NZ, Q_DEV, SLICE), BF16),
        in_specs=[
            pl.BlockSpec(parts.shape, lambda i: (0, 0, 0)),
            pl.BlockSpec((SLICE, width), lambda i: (i, 0)),
        ],
        out_specs=pl.BlockSpec((1, Q_DEV, SLICE), lambda i: (i, 0, 0)),
        scratch_shapes=[pltpu.VMEM((Q_DEV, width), BF16)],
        compiler_params=params(58),
        cost_estimate=pl.CostEstimate(flops=4 * 10**8, bytes_accessed=8 * 10**6, transcendentals=0),
        name="project",
    )(parts, weight)


def earlier():
    i = lax.broadcasted_iota(jnp.int32, (Q_DEV, Q_DEV), 0)
    j = lax.broadcasted_iota(jnp.int32, (Q_DEV, Q_DEV), 1)
    return i, j


def pack_kernel(heads_ref, own_ref, gain_ref, main_ref, over_ref, spread_ref, stream_ref, chunk_ref, made_ref, sems):
    summed = heads_ref[0].astype(F32)
    for z in range(1, NZ):
        summed = summed + heads_ref[z].astype(F32)
    stream = (own_ref[:, :SLICE].astype(F32) + summed).astype(BF16)
    stream_ref[...] = stream
    stream_f = stream.astype(F32)
    squares = stream_f * stream_f
    scaled = (stream_f * gain_ref[...]).astype(BF16)
    main = dot_nn(main_ref[...], scaled).astype(BF16)
    over = jnp.zeros((E * MAIN, THIRD), F32)
    for t in range(3):
        over = over + dot_nn(over_ref[t], scaled[:, t * THIRD : (t + 1) * THIRD])
    sums_row = dot_nt(jnp.ones((8, SLICE), F32), squares, precision=lax.Precision.HIGHEST)
    parts = jnp.concatenate(three_parts(sums_row), axis=0).astype(BF16)
    placed = dot_nt(parts, spread_ref[...])
    row = lax.broadcasted_iota(jnp.int32, (MAIN, HD), 0)
    for e in range(E):
        lanes = slice(e * HD, (e + 1) * HD)
        high, middle, low = placed[0:1, lanes], placed[8:9, lanes], placed[16:17, lanes]
        extra = jnp.where(
            row == 3 * OVER,
            high,
            jnp.where(row == 3 * OVER + 1, middle, jnp.where(row == 3 * OVER + 2, low, 0.0)),
        )
        here = slice(e * MAIN, (e + 1) * MAIN)
        begin = (over[here, :HD] + extra).astype(BF16)
        rest = over[here, HD:].astype(BF16)
        made_ref[e, :, :SLICE] = main[here]
        made_ref[e, :, SLICE : SLICE + HD] = begin
        made_ref[e, :, SLICE + HD :] = rest
    copies = [
        pltpu.make_async_copy(made_ref, chunk_ref.at[z, :, x], sems.at[z, x])
        for z in range(NZ)
        for x in range(2)
    ]
    for copy in copies:
        copy.start()
    for copy in copies:
        copy.wait()


def pack(heads, own, gain, main, over, spread):
    return pl.pallas_call(
        pack_kernel,
        out_shape=(
            jax.ShapeDtypeStruct((Q_DEV, SLICE), BF16),
            jax.ShapeDtypeStruct((NZ, E, 2, MAIN, CHUNK), BF16),
        ),
        in_specs=[VMEM] * 6,
        out_specs=(VMEM, HBM),
        scratch_shapes=[pltpu.VMEM((E, MAIN, CHUNK), BF16), pltpu.SemaphoreType.DMA((NZ, 2))],
        compiler_params=params(40),
        cost_estimate=pl.CostEstimate(flops=3 * 10**7, bytes_accessed=5 * 10**6, transcendentals=0),
        name="pack",
    )(heads, own, gain, main, over, spread)


RCV = PLANE * MAIN
F_BLOCK = 256
EXT = PLANE * OVER
ALL = RCV + EXT
def iotas(rows, cols):
    return (
        lax.broadcasted_iota(jnp.int32, (rows, cols), 0),
        lax.broadcasted_iota(jnp.int32, (rows, cols), 1),
    )


def unpack(x_ref, rows_ref):
    over_row, line = iotas(EXT, RCV)
    extra_sum = jnp.zeros((RCV, HD), F32)
    for z in range(NZ):
        rows_ref[:RCV, z * SLICE : (z + 1) * SLICE] = x_ref[z, :, :SLICE]
        over = x_ref[z, :, SLICE:]
        extra_sum = extra_sum + over[:, :HD].astype(F32)
        for t in range(3):
            pick = (line // MAIN == over_row // OVER) & (line % MAIN == t * OVER + over_row % OVER)
            rows_ref[RCV:, z * SLICE + t * THIRD : z * SLICE + (t + 1) * THIRD] = dot_nn(
                jnp.where(pick, 1.0, 0.0).astype(BF16), over
            ).astype(BF16)

    source, line = iotas(PLANE, RCV)
    part = line % MAIN
    pick = (line // MAIN == source) & (part >= 3 * OVER) & (part < 3 * OVER + 3)
    sums = dot_nn(jnp.where(pick, 1.0, 0.0), extra_sum, precision=lax.Precision.HIGHEST)
    row, source = iotas(ALL, PLANE)
    owner = jnp.where(row < RCV, row // MAIN, (row - RCV) // OVER)
    spread = dot_nn(jnp.where(owner == source, 1.0, 0.0), sums, precision=lax.Precision.HIGHEST)
    row, lane = iotas(ALL, HD)
    slot = jnp.where(row < RCV, row % MAIN, MAIN + (row - RCV) % OVER)
    column = jnp.sum(jnp.where(lane == slot, spread, 0.0), axis=1, keepdims=True)
    return lax.rsqrt(column * (1.0 / D) + NORM_EPS)


def repack(answer, made_ref, z):
    width = answer.shape[1]
    made_ref[z, :, :width] = answer[:RCV]
    line, over_row = iotas(RCV, EXT)
    for third in range(width // THIRD):
        over = jnp.zeros((RCV, HD), F32)
        for t in range(3):
            pick = (line // MAIN == over_row // OVER) & (line % MAIN == t * OVER + over_row % OVER)
            at = third * THIRD + t * HD
            over = over + dot_nn(jnp.where(pick, 1.0, 0.0).astype(BF16), answer[RCV:, at : at + HD])
        made_ref[z, :, width + third * HD : width + (third + 1) * HD] = over.astype(BF16)


AHEAD = 2
SLOTS = AHEAD + 1


def experts_kernel(
    x_any, ga_hbm, gb_hbm, ua_hbm, ub_hbm, da_hbm, db_hbm, out_hbm,
    made_ref, rows_ref, scale_ref, hidden_ref, gate_ref, up_ref, down_ref, x_sem, weight_sem, down_sem, out_sem,
):
    steps = ga_hbm.shape[1] // F_BLOCK

    def weight_copies(step, gate_hbm, up_hbm, block):
        cols = pl.ds(pl.multiple_of(block * F_BLOCK, F_BLOCK), F_BLOCK)
        slot = lax.rem(step, SLOTS)
        return (
            pltpu.make_async_copy(gate_hbm.at[:, cols], gate_ref.at[slot], weight_sem.at[0, slot]),
            pltpu.make_async_copy(up_hbm.at[:, cols], up_ref.at[slot], weight_sem.at[1, slot]),
        )

    def down_copies():
        return [
            [
                pltpu.make_async_copy(
                    hbm.at[:, z * SLICE : (z + 1) * SLICE], down_ref.at[side, z], down_sem.at[side, z]
                )
                for side, hbm in enumerate((da_hbm, db_hbm))
            ]
            for z in range(NZ)
        ]

    arrive = pltpu.make_async_copy(x_any, made_ref, x_sem)
    arrive.start()
    for step in range(AHEAD):
        for copy in weight_copies(step, ga_hbm, ua_hbm, step):
            copy.start()
    arrive.wait()
    scale_ref[...] = jnp.broadcast_to(unpack(made_ref, rows_ref), (ALL, HD))

    @pl.loop(0, 2 * steps)
    def _(step):
        later = step + AHEAD

        @pl.when(later < steps)
        def _():
            for copy in weight_copies(later, ga_hbm, ua_hbm, later):
                copy.start()

        @pl.when((later >= steps) & (later < 2 * steps))
        def _():
            for copy in weight_copies(later, gb_hbm, ub_hbm, later - steps):
                copy.start()

        @pl.when(later == 2 * steps)
        def _():
            for pair in down_copies():
                for copy in pair:
                    copy.start()

        for copy in weight_copies(step, ga_hbm, ua_hbm, 0):
            copy.wait()
        slot = lax.rem(step, SLOTS)
        gate = dot_nn(rows_ref[...], gate_ref[slot]) * scale_ref[:, :1]
        up = dot_nn(rows_ref[...], up_ref[slot]) * scale_ref[:, :1]
        to = pl.ds(pl.multiple_of(step * F_BLOCK, F_BLOCK), F_BLOCK)
        hidden_ref[:, to] = (gate / (1.0 + jnp.exp(-gate)) * up).astype(BF16)

    half = da_hbm.shape[0]
    sent = []
    for z, pair in enumerate(down_copies()):
        for copy in pair:
            copy.wait()
        answer = dot_nn(hidden_ref[:, :half], down_ref[0, z]) + dot_nn(hidden_ref[:, half:], down_ref[1, z])
        repack(answer.astype(BF16), made_ref, z)
        sent.append(pltpu.make_async_copy(made_ref.at[z], out_hbm.at[z], out_sem.at[z]))
        sent[-1].start()
    for copy in sent:
        copy.wait()


def experts(x, ga, gb, ua, ub, da, db):
    width = ga.shape[1]
    return pl.pallas_call(
        experts_kernel,
        out_shape=jax.ShapeDtypeStruct(x.shape, BF16),
        in_specs=[ANY] + [HBM] * 6,
        out_specs=HBM,
        scratch_shapes=[
            pltpu.VMEM(x.shape, BF16),
            pltpu.VMEM((ALL, D), BF16),
            pltpu.VMEM((ALL, HD), F32),
            pltpu.VMEM((ALL, 2 * width), BF16),
            pltpu.VMEM((SLOTS, D, F_BLOCK), BF16),
            pltpu.VMEM((SLOTS, D, F_BLOCK), BF16),
            pltpu.VMEM((2, NZ, width, SLICE), BF16),
            pltpu.SemaphoreType.DMA,
            pltpu.SemaphoreType.DMA((2, SLOTS)),
            pltpu.SemaphoreType.DMA((2, NZ)),
            pltpu.SemaphoreType.DMA((NZ,)),
        ],
        compiler_params=params(56),
        cost_estimate=pl.CostEstimate(flops=14 * 10**9, bytes_accessed=48 * 10**6, transcendentals=10**6),
        name="experts",
    )(x, ga, gb, ua, ub, da, db)


def place_rows(codes, main_ref, over_ref, spread_ref):
    kind, lane = iotas(8, PACK)
    turned = dot_nt(jnp.where(kind == lane, 1.0, 0.0).astype(BF16), codes)
    first, second = turned[0:1, :], turned[1:2, :]
    expert = lax.broadcasted_iota(jnp.int32, (E, Q_DEV), 0).astype(F32)
    hot0 = jnp.where(expert == first, 1.0, 0.0)
    hot1 = jnp.where(expert == second, 1.0, 0.0)
    j, i = earlier()
    before_t = jnp.where((j < i) & (j // 16 == i // 16), 1.0, 0.0)
    counts = dot_nn((hot0 + hot1).astype(BF16), before_t.astype(BF16))
    base = (lax.broadcasted_iota(jnp.int32, (1, Q_DEV), 1) // 16 * CAP).astype(F32)
    slot0 = jnp.sum(counts * hot0, axis=0, keepdims=True) + base
    slot1 = jnp.sum(counts * hot1, axis=0, keepdims=True) + base

    def placing(slot, which):
        hit = ((slot == slot0) & (which == first)) | ((slot == slot1) & (which == second))
        return jnp.where(hit, 1.0, 0.0).astype(BF16)

    line = lax.broadcasted_iota(jnp.int32, (E * MAIN, Q_DEV), 0)
    which = (line // MAIN).astype(F32)
    part = line % MAIN
    main_ref[...] = placing(part.astype(F32), which)
    for t in range(3):
        over_ref[t] = placing(jnp.where(part // OVER == t, MAIN + part % OVER, -1).astype(F32), which)
    line = lax.broadcasted_iota(jnp.int32, (E * HD, Q_DEV), 0)
    spread_ref[...] = placing((line % HD).astype(F32), (line // HD).astype(F32))


def routing_kernel(own_ref, main_ref, over_ref, spread_ref, mix_ref):
    codes = own_ref[:, SLICE:]
    place_rows(codes, main_ref, over_ref, spread_ref)
    routes_ref = codes.astype(F32)
    first, second = routes_ref[:, 0:1], routes_ref[:, 1:2]
    weight0 = routes_ref[:, 2:3] + routes_ref[:, 3:4] + routes_ref[:, 4:5]
    weight1 = routes_ref[:, 5:6] + routes_ref[:, 6:7] + routes_ref[:, 7:8]
    expert = lax.broadcasted_iota(jnp.int32, (Q_DEV, HD), 1).astype(F32)
    hot0 = jnp.where(expert == first, 1.0, 0.0)
    hot1 = jnp.where(expert == second, 1.0, 0.0)
    i, j = earlier()
    before = jnp.where((j < i) & (j // 16 == i // 16), 1.0, 0.0)
    counts = dot_nn(before.astype(BF16), (hot0 + hot1).astype(BF16))
    base = (lax.broadcasted_iota(jnp.int32, (Q_DEV, 1), 0) // 16 * CAP).astype(F32)
    slot0 = jnp.sum(counts * hot0, axis=1, keepdims=True) + base
    slot1 = jnp.sum(counts * hot1, axis=1, keepdims=True) + base
    col = lax.broadcasted_iota(jnp.int32, (Q_DEV, RCV), 1)
    part = col % MAIN
    which = (col // (2 * MAIN)).astype(F32)
    for kind in range(4):
        slot = part if kind == 0 else jnp.where(part // OVER == kind - 1, MAIN + part % OVER, -1)
        slot = slot.astype(F32)
        mix = jnp.where((slot == slot0) & (which == first), weight0, 0.0) + jnp.where(
            (slot == slot1) & (which == second), weight1, 0.0
        )
        for at, value in enumerate(three_parts(mix)):
            mix_ref[kind, at * Q_DEV : (at + 1) * Q_DEV, :] = value.astype(BF16)


def routing(own):
    return pl.pallas_call(
        routing_kernel,
        out_shape=(
            jax.ShapeDtypeStruct((E * MAIN, Q_DEV), BF16),
            jax.ShapeDtypeStruct((3, E * MAIN, Q_DEV), BF16),
            jax.ShapeDtypeStruct((E * HD, Q_DEV), BF16),
            jax.ShapeDtypeStruct((4, 3 * Q_DEV, RCV), BF16),
        ),
        compiler_params=params(30),
        cost_estimate=pl.CostEstimate(flops=10**6, bytes_accessed=10**6, transcendentals=0),
        name="routing",
    )(own)


def combine_kernel(returned_hbm, stream_ref, mix_ref, out_ref, returned_ref, sems):
    copies = [
        pltpu.make_async_copy(returned_hbm.at[z], returned_ref.at[z], sems.at[z]) for z in range(NZ)
    ]
    for copy in copies:
        copy.start()

    def fold(kind, block):
        moved = dot_nn(mix_ref[kind], block)
        return moved[:Q_DEV] + moved[Q_DEV : 2 * Q_DEV] + moved[2 * Q_DEV :]

    total = stream_ref[...].astype(F32)
    extra = [jnp.zeros((Q_DEV, HD), F32)] * (SLICE // HD)
    for z in range(NZ):
        copies[z].wait()
        total = total + fold(0, returned_ref[z, :, :SLICE])
        for at in range(SLICE // HD):
            lanes = slice(SLICE + at // 3 * HD, SLICE + (at // 3 + 1) * HD)
            extra[at] = extra[at] + fold(at % 3 + 1, returned_ref[z, :, lanes])
    for at, part in enumerate(extra):
        cols = slice(at * HD, (at + 1) * HD)
        out_ref[:, cols] = (total[:, cols] + part).astype(BF16)


def combine(returned, stream, mix):
    return pl.pallas_call(
        combine_kernel,
        out_shape=jax.ShapeDtypeStruct((Q_DEV, SLICE), BF16),
        in_specs=[ANY, VMEM, VMEM],
        out_specs=VMEM,
        scratch_shapes=[pltpu.VMEM(returned.shape, BF16), pltpu.SemaphoreType.DMA((NZ,))],
        compiler_params=params(40),
        cost_estimate=pl.CostEstimate(flops=7 * 10**8, bytes_accessed=5 * 10**6, transcendentals=0),
        name="combine",
    )(returned, stream, mix)


def body(
    residual,
    queries,
    new_keys,
    new_values,
    cache_keys,
    cache_values,
    out_weight,
    norm_gain,
    route_ids,
    route_weight,
    gate_weight,
    up_weight,
    down_weight,
):
    core = lax.axis_index("c")
    mine = lax.axis_index(XY) * 2 + core
    depth = lax.axis_index("z")

    head_width = HEADS * HD
    far_keys = other_core(cache_keys)
    far_values = other_core(cache_values)
    far_new_keys = other_core(new_keys)
    far_new_values = other_core(new_values)
    weight_t = lax.all_gather(out_weight.T, XY + ("c",), axis=0, tiled=True)
    all_queries = exchange(jnp.broadcast_to(queries[None], (PLANE, Q_DEV, head_width)), XY)
    tok = residual.shape[0]
    codes = jnp.concatenate(
        [
            route_ids.astype(F32),
            jnp.stack(three_parts(route_weight[:, 0]) + three_parts(route_weight[:, 1]), axis=1),
        ],
        axis=1,
    ).astype(BF16)
    codes = jnp.pad(codes, ((0, 0), (0, PACK - codes.shape[1])))
    own = jnp.transpose(residual.reshape(tok, NZ, SLICE), (1, 0, 2))
    own = jnp.concatenate([own, jnp.broadcast_to(codes[None], (NZ, tok, PACK))], axis=2)
    own = around_z(own, depth).reshape(Q_DEV, SLICE + PACK)
    main, over, spread, mix = routing(own)
    mix, all_queries = lax.optimization_barrier((mix, all_queries))

    place = jnp.stack([core, mine]).astype(jnp.int32)
    partial = attend(
        place, all_queries, cache_keys, far_keys, new_keys, far_new_keys,
        cache_values, far_values, new_values, far_new_values,
    )
    after = lax.optimization_barrier((gate_weight, up_weight, down_weight, all_queries))
    far_gate, far_up, far_down = (other_core(w) for w in after[:3])
    parts = exchange(partial, XY)
    heads = exchange(project(parts, weight_t), ("z",))
    gain = lax.dynamic_slice_in_dim(norm_gain, depth * SLICE, SLICE, 0)[None]
    stream, chunks = pack(heads, own, gain, main, over, spread)
    arrived = exchange(chunks.reshape(NZ * PLANE, MAIN, CHUNK), ZXY).reshape(NZ, RCV, CHUNK)
    answers = experts(arrived, gate_weight, far_gate, up_weight, far_up, down_weight, far_down)
    returned = exchange(answers.reshape(NZ * PLANE, MAIN, CHUNK), ZXY).reshape(NZ, RCV, CHUNK)
    layer = combine(returned, stream, mix)
    final = exchange(layer.reshape(NZ, tok, SLICE), ("z",))
    return jnp.transpose(final, (1, 0, 2)).reshape(tok, D)


def solution(mesh):
    split = Mesh(mesh.devices.reshape(4, 2, 2, 2, NZ), ("y", "xh", "xl", "c", "z"))
    dp = ("y", "xh", "xl", "c")
    rows = dp + ("z",)
    placed = (
        P(rows, None),
        P(dp, "z"),
        P(dp, "z"),
        P(dp, "z"),
        P(dp, "z"),
        P(dp, "z"),
        P("z", dp),
        P(),
        P(rows, None),
        P(rows, None),
        P(None, rows),
        P(None, rows),
        P(rows, None),
    )
    return jax.shard_map(body, mesh=split, in_specs=placed, out_specs=P(rows, None), check_vma=False)
```

```python
import functools
import math

import jax
import jax.numpy as jnp
from jax import lax
from jax.experimental import pallas as pl
from jax.experimental.pallas import tpu as pltpu
from jax.sharding import Mesh, PartitionSpec as P

D = 4608
HD = 128
HEADS = 5
E = 8
TOP = 2
CAP = 5
NZ = 4
PLANE = 16
Q_DEV = 64
SLICE = D // NZ
MAIN = 16
OVER = NZ * CAP - MAIN
THIRD = SLICE // 3
CHUNK = SLICE + THIRD
PACK = 128
LINES = HEADS * Q_DEV + 8
NORM_EPS = 1e-06
NEGATIVE = -1e30
TO_BASE2 = math.log2(math.e) / math.sqrt(HD)

XY = ("y", "xh", "xl")
ZXY = ("z", "y", "xh", "xl")
F32 = jnp.float32
BF16 = jnp.bfloat16


VMEM = pl.BlockSpec(memory_space=pltpu.VMEM)
HBM = pl.BlockSpec(memory_space=pltpu.HBM)
ANY = pl.BlockSpec(memory_space=pl.ANY)


def params(mib):
    return pltpu.CompilerParams(vmem_limit_bytes=mib * 2**20)


def exchange(block, axes):
    return lax.all_to_all(block, axes, split_axis=0, concat_axis=0, tiled=True)


def other_core(block):
    return lax.ppermute(block, "c", [(0, 1), (1, 0)])


def around_z(blocks, depth):
    take = lambda a, i: lax.dynamic_index_in_dim(a, i % NZ, 0, keepdims=False)
    got = [take(blocks, depth)]
    for step in range(1, NZ):
        route = [(i, (i + step) % NZ) for i in range(NZ)]
        got.append(lax.ppermute(take(blocks, depth + step), "z", route))
    got = jnp.stack(got)
    return jnp.stack([take(got, depth - i + NZ) for i in range(NZ)])


def three_parts(value):
    high = value.astype(BF16).astype(F32)
    rest = value - high
    middle = rest.astype(BF16).astype(F32)
    return high, middle, (rest - middle).astype(BF16).astype(F32)


def dot_nt(a, b, **kw):
    return lax.dot_general(a, b, (((1,), (1,)), ((), ())), preferred_element_type=F32, **kw)


def dot_nn(a, b, **kw):
    return lax.dot_general(a, b, (((1,), (0,)), ((), ())), preferred_element_type=F32, **kw)


Q_BLOCKS = 8


def attend_kernel(place_ref, q_ref, ka_ref, kb_ref, na_ref, nb_ref, va_ref, vb_ref, wa_ref, wb_ref, out_ref):
    core, mine = place_ref[0], place_ref[1]
    rows = Q_BLOCKS * Q_DEV
    row = lax.broadcasted_iota(jnp.int32, (rows, HD), 0)
    lane = lax.broadcasted_iota(jnp.int32, (rows, HD), 1)
    block = pl.program_id(0) * Q_BLOCKS + row // Q_DEV
    q_pos = (block * 2 + core) * Q_DEV + row % Q_DEV
    k_pos = jnp.where(lane < Q_DEV, mine * Q_DEV + lane, (mine + 1 - 2 * core) * Q_DEV + lane - Q_DEV)
    allowed = k_pos <= q_pos
    pack = jnp.zeros((rows, PACK), F32)
    group = row % Q_DEV // 8 * 16
    for h in range(HEADS):
        cols = slice(h * HD, (h + 1) * HD)
        q = q_ref[:, :, cols].reshape(rows, HD)
        s1 = dot_nt(q, ka_ref[:, cols])
        s2 = dot_nt(q, kb_ref[:, cols])
        fresh = jnp.concatenate([na_ref[:, cols], nb_ref[:, cols]], axis=0)
        s3 = jnp.where(allowed, dot_nt(q, fresh), NEGATIVE)
        top = jnp.maximum(
            jnp.maximum(jnp.max(s1, axis=1, keepdims=True), jnp.max(s2, axis=1, keepdims=True)),
            jnp.max(s3, axis=1, keepdims=True),
        ) * TO_BASE2
        w1 = jnp.exp2(s1 * TO_BASE2 - top)
        w2 = jnp.exp2(s2 * TO_BASE2 - top)
        w3 = jnp.exp2(s3 * TO_BASE2 - top)
        total = (
            jnp.sum(w1, axis=1, keepdims=True)
            + jnp.sum(w2, axis=1, keepdims=True)
            + jnp.sum(w3, axis=1, keepdims=True)
        )
        fresh_v = jnp.concatenate([wa_ref[:, cols], wb_ref[:, cols]], axis=0)
        acc = (
            dot_nn(w1.astype(BF16), va_ref[:, cols])
            + dot_nn(w2.astype(BF16), vb_ref[:, cols])
            + dot_nn(w3.astype(BF16), fresh_v)
        )
        out_ref[:, h * Q_DEV : (h + 1) * Q_DEV, :] = (
            (acc / total).astype(BF16).reshape(Q_BLOCKS, Q_DEV, HD)
        )
        for part, value in enumerate(three_parts(top + jnp.log2(total))):
            pack = jnp.where(lane == group + part * HEADS + h, value, pack)
    folded = jnp.sum(pack.reshape(Q_BLOCKS, 8, 8, PACK), axis=1)
    out_ref[:, HEADS * Q_DEV :, :] = folded.astype(BF16)


def attend(place, q, *keys):
    whole = [pl.BlockSpec(a.shape, lambda i: (0, 0)) for a in keys]
    return pl.pallas_call(
        attend_kernel,
        grid=(PLANE // Q_BLOCKS,),
        out_shape=jax.ShapeDtypeStruct((PLANE, LINES, HD), BF16),
        in_specs=[
            pl.BlockSpec(memory_space=pltpu.SMEM),
            pl.BlockSpec((Q_BLOCKS, Q_DEV, HEADS * HD), lambda i: (i, 0, 0)),
            *whole,
        ],
        out_specs=pl.BlockSpec((Q_BLOCKS, LINES, HD), lambda i: (i, 0, 0)),
        compiler_params=params(56),
        cost_estimate=pl.CostEstimate(flops=11 * 10**9, bytes_accessed=10**7, transcendentals=11 * 10**6),
        name="attend",
    )(place, q, *keys)


def merge(parts_ref, out_ref):
    count = parts_ref.shape[0]
    sums = [parts_ref[i, HEADS * Q_DEV :, :].astype(F32) for i in range(count)]
    sums = [
        s + pltpu.roll(s, PACK - HEADS, axis=1) + pltpu.roll(s, PACK - 2 * HEADS, axis=1) for s in sums
    ]
    for h in range(HEADS):
        logs = [
            jnp.concatenate([s[:, g * 16 + h : g * 16 + h + 1] for g in range(8)], axis=0) for s in sums
        ]
        top = functools.reduce(jnp.maximum, logs)
        shares = [jnp.exp2(v - top) for v in logs]
        total = functools.reduce(jnp.add, shares)
        acc = functools.reduce(
            jnp.add,
            [
                shares[i] * parts_ref[i, h * Q_DEV : (h + 1) * Q_DEV, :].astype(F32)
                for i in range(count)
            ],
        )
        out_ref[:, h * HD : (h + 1) * HD] = (acc / total).astype(BF16)


def project_kernel(parts_ref, weight_hbm, out_ref, attended_ref, weight_ref, sems):
    pieces = [
        pltpu.make_async_copy(
            weight_hbm.at[z * SLICE : (z + 1) * SLICE, :], weight_ref.at[z], sems.at[z]
        )
        for z in range(NZ)
    ]
    for piece in pieces:
        piece.start()
    merge(parts_ref, attended_ref)
    for z, piece in enumerate(pieces):
        piece.wait()
        out_ref[z] = dot_nt(attended_ref[...], weight_ref[z]).astype(BF16)


def project(parts, weight):
    width = HEADS * HD
    return pl.pallas_call(
        project_kernel,
        out_shape=jax.ShapeDtypeStruct((NZ, Q_DEV, SLICE), BF16),
        in_specs=[VMEM, HBM],
        out_specs=VMEM,
        scratch_shapes=[
            pltpu.VMEM((Q_DEV, width), BF16),
            pltpu.VMEM((NZ, SLICE, width), BF16),
            pltpu.SemaphoreType.DMA((NZ,)),
        ],
        compiler_params=params(56),
        cost_estimate=pl.CostEstimate(flops=4 * 10**8, bytes_accessed=8 * 10**6, transcendentals=0),
        name="project",
    )(parts, weight)


def earlier():
    i = lax.broadcasted_iota(jnp.int32, (Q_DEV, Q_DEV), 0)
    j = lax.broadcasted_iota(jnp.int32, (Q_DEV, Q_DEV), 1)
    return i, j


def pack_kernel(heads_ref, own_ref, gain_ref, main_ref, over_ref, spread_ref, stream_ref, chunk_ref, made_ref, sems):
    summed = heads_ref[0].astype(F32)
    for z in range(1, NZ):
        summed = summed + heads_ref[z].astype(F32)
    stream = (own_ref[:, :SLICE].astype(F32) + summed).astype(BF16)
    stream_ref[...] = stream
    stream_f = stream.astype(F32)
    squares = stream_f * stream_f
    scaled = (stream_f * gain_ref[...]).astype(BF16)
    main = dot_nn(main_ref[...], scaled).astype(BF16)
    over = jnp.zeros((E * MAIN, THIRD), F32)
    for t in range(3):
        over = over + dot_nn(over_ref[t], scaled[:, t * THIRD : (t + 1) * THIRD])
    sums_row = dot_nt(jnp.ones((8, SLICE), F32), squares, precision=lax.Precision.HIGHEST)
    parts = jnp.concatenate(three_parts(sums_row), axis=0).astype(BF16)
    placed = dot_nt(parts, spread_ref[...])
    row = lax.broadcasted_iota(jnp.int32, (MAIN, HD), 0)
    for e in range(E):
        lanes = slice(e * HD, (e + 1) * HD)
        high, middle, low = placed[0:1, lanes], placed[8:9, lanes], placed[16:17, lanes]
        extra = jnp.where(
            row == 3 * OVER,
            high,
            jnp.where(row == 3 * OVER + 1, middle, jnp.where(row == 3 * OVER + 2, low, 0.0)),
        )
        here = slice(e * MAIN, (e + 1) * MAIN)
        begin = (over[here, :HD] + extra).astype(BF16)
        rest = over[here, HD:].astype(BF16)
        made_ref[e, :, :SLICE] = main[here]
        made_ref[e, :, SLICE : SLICE + HD] = begin
        made_ref[e, :, SLICE + HD :] = rest
    copies = [
        pltpu.make_async_copy(made_ref, chunk_ref.at[z, :, x], sems.at[z, x])
        for z in range(NZ)
        for x in range(2)
    ]
    for copy in copies:
        copy.start()
    for copy in copies:
        copy.wait()


def pack(heads, own, gain, main, over, spread):
    return pl.pallas_call(
        pack_kernel,
        out_shape=(
            jax.ShapeDtypeStruct((Q_DEV, SLICE), BF16),
            jax.ShapeDtypeStruct((NZ, E, 2, MAIN, CHUNK), BF16),
        ),
        in_specs=[VMEM] * 6,
        out_specs=(VMEM, HBM),
        scratch_shapes=[pltpu.VMEM((E, MAIN, CHUNK), BF16), pltpu.SemaphoreType.DMA((NZ, 2))],
        compiler_params=params(40),
        cost_estimate=pl.CostEstimate(flops=3 * 10**7, bytes_accessed=5 * 10**6, transcendentals=0),
        name="pack",
    )(heads, own, gain, main, over, spread)


RCV = PLANE * MAIN
F_BLOCK = 256
EXT = PLANE * OVER
ALL = RCV + EXT
def iotas(rows, cols):
    return (
        lax.broadcasted_iota(jnp.int32, (rows, cols), 0),
        lax.broadcasted_iota(jnp.int32, (rows, cols), 1),
    )


def unpack(x_ref, rows_ref):
    over_row, line = iotas(EXT, RCV)
    extra_sum = jnp.zeros((RCV, HD), F32)
    for z in range(NZ):
        rows_ref[:RCV, z * SLICE : (z + 1) * SLICE] = x_ref[z, :, :SLICE]
        over = x_ref[z, :, SLICE:]
        extra_sum = extra_sum + over[:, :HD].astype(F32)
        for t in range(3):
            pick = (line // MAIN == over_row // OVER) & (line % MAIN == t * OVER + over_row % OVER)
            rows_ref[RCV:, z * SLICE + t * THIRD : z * SLICE + (t + 1) * THIRD] = dot_nn(
                jnp.where(pick, 1.0, 0.0).astype(BF16), over
            ).astype(BF16)

    source, line = iotas(PLANE, RCV)
    part = line % MAIN
    pick = (line // MAIN == source) & (part >= 3 * OVER) & (part < 3 * OVER + 3)
    sums = dot_nn(jnp.where(pick, 1.0, 0.0), extra_sum, precision=lax.Precision.HIGHEST)
    row, source = iotas(ALL, PLANE)
    owner = jnp.where(row < RCV, row // MAIN, (row - RCV) // OVER)
    spread = dot_nn(jnp.where(owner == source, 1.0, 0.0), sums, precision=lax.Precision.HIGHEST)
    row, lane = iotas(ALL, HD)
    slot = jnp.where(row < RCV, row % MAIN, MAIN + (row - RCV) % OVER)
    column = jnp.sum(jnp.where(lane == slot, spread, 0.0), axis=1, keepdims=True)
    return lax.rsqrt(column * (1.0 / D) + NORM_EPS)


def repack(answer, made_ref, z):
    width = answer.shape[1]
    made_ref[z, :, :width] = answer[:RCV]
    line, over_row = iotas(RCV, EXT)
    for third in range(width // THIRD):
        over = jnp.zeros((RCV, HD), F32)
        for t in range(3):
            pick = (line // MAIN == over_row // OVER) & (line % MAIN == t * OVER + over_row % OVER)
            at = third * THIRD + t * HD
            over = over + dot_nn(jnp.where(pick, 1.0, 0.0).astype(BF16), answer[RCV:, at : at + HD])
        made_ref[z, :, width + third * HD : width + (third + 1) * HD] = over.astype(BF16)


AHEAD = 2
SLOTS = AHEAD + 1


def experts_kernel(
    x_any, ga_hbm, gb_hbm, ua_hbm, ub_hbm, da_hbm, db_hbm, out_hbm,
    made_ref, rows_ref, scale_ref, hidden_ref, both_ref, down_ref, x_sem, weight_sem, down_sem, out_sem,
):
    half = da_hbm.shape[0]
    steps = half // F_BLOCK

    def weight_copies(step, gate_hbm, up_hbm, block):
        cols = pl.ds(pl.multiple_of(block * F_BLOCK, F_BLOCK), F_BLOCK)
        slot = lax.rem(step, SLOTS)
        return (
            pltpu.make_async_copy(gate_hbm.at[:, cols], both_ref.at[slot, :, :F_BLOCK], weight_sem.at[0, slot]),
            pltpu.make_async_copy(up_hbm.at[:, cols], both_ref.at[slot, :, F_BLOCK:], weight_sem.at[1, slot]),
        )

    def down_copies():
        return [
            [
                pltpu.make_async_copy(
                    hbm.at[:, z * SLICE : (z + 1) * SLICE],
                    down_ref.at[z, side * half : (side + 1) * half, :],
                    down_sem.at[side, z],
                )
                for side, hbm in enumerate((da_hbm, db_hbm))
            ]
            for z in range(NZ)
        ]

    arrive = pltpu.make_async_copy(x_any, made_ref, x_sem)
    arrive.start()
    for step in range(AHEAD):
        for copy in weight_copies(step, ga_hbm, ua_hbm, step):
            copy.start()
    arrive.wait()
    scale_ref[...] = jnp.broadcast_to(unpack(made_ref, rows_ref), (ALL, HD))

    @pl.loop(0, 2 * steps)
    def _(step):
        later = step + AHEAD

        @pl.when(later < steps)
        def _():
            for copy in weight_copies(later, ga_hbm, ua_hbm, later):
                copy.start()

        @pl.when((later >= steps) & (later < 2 * steps))
        def _():
            for copy in weight_copies(later, gb_hbm, ub_hbm, later - steps):
                copy.start()

        @pl.when(later == 2 * steps)
        def _():
            for pair in down_copies():
                for copy in pair:
                    copy.start()

        for copy in weight_copies(step, ga_hbm, ua_hbm, 0):
            copy.wait()
        slot = lax.rem(step, SLOTS)
        both = dot_nn(rows_ref[...], both_ref[slot]) * scale_ref[:, :1]
        gate, up = both[:, :F_BLOCK], both[:, F_BLOCK:]
        to = pl.ds(pl.multiple_of(step * F_BLOCK, F_BLOCK), F_BLOCK)
        hidden_ref[:, to] = (gate / (1.0 + jnp.exp(-gate)) * up).astype(BF16)

    sent = []
    for z, pair in enumerate(down_copies()):
        for copy in pair:
            copy.wait()
        repack(dot_nn(hidden_ref[...], down_ref[z]).astype(BF16), made_ref, z)
        sent.append(pltpu.make_async_copy(made_ref.at[z], out_hbm.at[z], out_sem.at[z]))
        sent[-1].start()
    for copy in sent:
        copy.wait()


def experts(x, ga, gb, ua, ub, da, db):
    width = ga.shape[1]
    return pl.pallas_call(
        experts_kernel,
        out_shape=jax.ShapeDtypeStruct(x.shape, BF16),
        in_specs=[ANY] + [HBM] * 6,
        out_specs=HBM,
        scratch_shapes=[
            pltpu.VMEM(x.shape, BF16),
            pltpu.VMEM((ALL, D), BF16),
            pltpu.VMEM((ALL, HD), F32),
            pltpu.VMEM((ALL, 2 * width), BF16),
            pltpu.VMEM((SLOTS, D, 2 * F_BLOCK), BF16),
            pltpu.VMEM((NZ, 2 * width, SLICE), BF16),
            pltpu.SemaphoreType.DMA,
            pltpu.SemaphoreType.DMA((2, SLOTS)),
            pltpu.SemaphoreType.DMA((2, NZ)),
            pltpu.SemaphoreType.DMA((NZ,)),
        ],
        compiler_params=params(56),
        cost_estimate=pl.CostEstimate(flops=14 * 10**9, bytes_accessed=48 * 10**6, transcendentals=10**6),
        name="experts",
    )(x, ga, gb, ua, ub, da, db)


def place_rows(codes, main_ref, over_ref, spread_ref):
    kind, lane = iotas(8, PACK)
    turned = dot_nt(jnp.where(kind == lane, 1.0, 0.0).astype(BF16), codes)
    first, second = turned[0:1, :], turned[1:2, :]
    expert = lax.broadcasted_iota(jnp.int32, (E, Q_DEV), 0).astype(F32)
    hot0 = jnp.where(expert == first, 1.0, 0.0)
    hot1 = jnp.where(expert == second, 1.0, 0.0)
    j, i = earlier()
    before_t = jnp.where((j < i) & (j // 16 == i // 16), 1.0, 0.0)
    counts = dot_nn((hot0 + hot1).astype(BF16), before_t.astype(BF16))
    base = (lax.broadcasted_iota(jnp.int32, (1, Q_DEV), 1) // 16 * CAP).astype(F32)
    slot0 = jnp.sum(counts * hot0, axis=0, keepdims=True) + base
    slot1 = jnp.sum(counts * hot1, axis=0, keepdims=True) + base

    def placing(slot, which):
        hit = ((slot == slot0) & (which == first)) | ((slot == slot1) & (which == second))
        return jnp.where(hit, 1.0, 0.0).astype(BF16)

    line = lax.broadcasted_iota(jnp.int32, (E * MAIN, Q_DEV), 0)
    which = (line // MAIN).astype(F32)
    part = line % MAIN
    main_ref[...] = placing(part.astype(F32), which)
    for t in range(3):
        over_ref[t] = placing(jnp.where(part // OVER == t, MAIN + part % OVER, -1).astype(F32), which)
    line = lax.broadcasted_iota(jnp.int32, (E * HD, Q_DEV), 0)
    spread_ref[...] = placing((line % HD).astype(F32), (line // HD).astype(F32))


def routing_kernel(own_ref, main_ref, over_ref, spread_ref, mix_ref):
    codes = own_ref[:, SLICE:]
    place_rows(codes, main_ref, over_ref, spread_ref)
    routes_ref = codes.astype(F32)
    first, second = routes_ref[:, 0:1], routes_ref[:, 1:2]
    weight0 = routes_ref[:, 2:3] + routes_ref[:, 3:4] + routes_ref[:, 4:5]
    weight1 = routes_ref[:, 5:6] + routes_ref[:, 6:7] + routes_ref[:, 7:8]
    expert = lax.broadcasted_iota(jnp.int32, (Q_DEV, HD), 1).astype(F32)
    hot0 = jnp.where(expert == first, 1.0, 0.0)
    hot1 = jnp.where(expert == second, 1.0, 0.0)
    i, j = earlier()
    before = jnp.where((j < i) & (j // 16 == i // 16), 1.0, 0.0)
    counts = dot_nn(before.astype(BF16), (hot0 + hot1).astype(BF16))
    base = (lax.broadcasted_iota(jnp.int32, (Q_DEV, 1), 0) // 16 * CAP).astype(F32)
    slot0 = jnp.sum(counts * hot0, axis=1, keepdims=True) + base
    slot1 = jnp.sum(counts * hot1, axis=1, keepdims=True) + base
    col = lax.broadcasted_iota(jnp.int32, (Q_DEV, RCV), 1)
    part = col % MAIN
    which = (col // (2 * MAIN)).astype(F32)
    for kind in range(4):
        slot = part if kind == 0 else jnp.where(part // OVER == kind - 1, MAIN + part % OVER, -1)
        slot = slot.astype(F32)
        mix = jnp.where((slot == slot0) & (which == first), weight0, 0.0) + jnp.where(
            (slot == slot1) & (which == second), weight1, 0.0
        )
        for at, value in enumerate(three_parts(mix)):
            mix_ref[kind, at * Q_DEV : (at + 1) * Q_DEV, :] = value.astype(BF16)


def routing(own):
    return pl.pallas_call(
        routing_kernel,
        out_shape=(
            jax.ShapeDtypeStruct((E * MAIN, Q_DEV), BF16),
            jax.ShapeDtypeStruct((3, E * MAIN, Q_DEV), BF16),
            jax.ShapeDtypeStruct((E * HD, Q_DEV), BF16),
            jax.ShapeDtypeStruct((4, 3 * Q_DEV, RCV), BF16),
        ),
        compiler_params=params(30),
        cost_estimate=pl.CostEstimate(flops=10**6, bytes_accessed=10**6, transcendentals=0),
        name="routing",
    )(own)


def combine_kernel(returned_hbm, stream_ref, mix_ref, out_ref, returned_ref, sems):
    copies = [
        pltpu.make_async_copy(returned_hbm.at[z], returned_ref.at[z], sems.at[z]) for z in range(NZ)
    ]
    for copy in copies:
        copy.start()

    def fold(kind, block):
        moved = dot_nn(mix_ref[kind], block)
        return moved[:Q_DEV] + moved[Q_DEV : 2 * Q_DEV] + moved[2 * Q_DEV :]

    total = stream_ref[...].astype(F32)
    extra = [jnp.zeros((Q_DEV, HD), F32)] * (SLICE // HD)
    for z in range(NZ):
        copies[z].wait()
        total = total + fold(0, returned_ref[z, :, :SLICE])
        for at in range(SLICE // HD):
            lanes = slice(SLICE + at // 3 * HD, SLICE + (at // 3 + 1) * HD)
            extra[at] = extra[at] + fold(at % 3 + 1, returned_ref[z, :, lanes])
    for at, part in enumerate(extra):
        cols = slice(at * HD, (at + 1) * HD)
        out_ref[:, cols] = (total[:, cols] + part).astype(BF16)


def combine(returned, stream, mix):
    return pl.pallas_call(
        combine_kernel,
        out_shape=jax.ShapeDtypeStruct((Q_DEV, SLICE), BF16),
        in_specs=[ANY, VMEM, VMEM],
        out_specs=VMEM,
        scratch_shapes=[pltpu.VMEM(returned.shape, BF16), pltpu.SemaphoreType.DMA((NZ,))],
        compiler_params=params(40),
        cost_estimate=pl.CostEstimate(flops=7 * 10**8, bytes_accessed=5 * 10**6, transcendentals=0),
        name="combine",
    )(returned, stream, mix)


def body(
    residual,
    queries,
    new_keys,
    new_values,
    cache_keys,
    cache_values,
    out_weight,
    norm_gain,
    route_ids,
    route_weight,
    gate_weight,
    up_weight,
    down_weight,
):
    core = lax.axis_index("c")
    mine = lax.axis_index(XY) * 2 + core
    depth = lax.axis_index("z")

    head_width = HEADS * HD
    far_keys = other_core(cache_keys)
    far_values = other_core(cache_values)
    far_new_keys = other_core(new_keys)
    far_new_values = other_core(new_values)
    weight_t = lax.all_gather(out_weight.T, XY + ("c",), axis=0, tiled=True)
    all_queries = exchange(jnp.broadcast_to(queries[None], (PLANE, Q_DEV, head_width)), XY)
    tok = residual.shape[0]
    codes = jnp.concatenate(
        [
            route_ids.astype(F32),
            jnp.stack(three_parts(route_weight[:, 0]) + three_parts(route_weight[:, 1]), axis=1),
        ],
        axis=1,
    ).astype(BF16)
    codes = jnp.pad(codes, ((0, 0), (0, PACK - codes.shape[1])))
    own = jnp.transpose(residual.reshape(tok, NZ, SLICE), (1, 0, 2))
    own = jnp.concatenate([own, jnp.broadcast_to(codes[None], (NZ, tok, PACK))], axis=2)
    own = around_z(own, depth).reshape(Q_DEV, SLICE + PACK)
    main, over, spread, mix = routing(own)
    mix, all_queries = lax.optimization_barrier((mix, all_queries))

    place = jnp.stack([core, mine]).astype(jnp.int32)
    partial = attend(
        place, all_queries, cache_keys, far_keys, new_keys, far_new_keys,
        cache_values, far_values, new_values, far_new_values,
    )
    after = lax.optimization_barrier((gate_weight, up_weight, down_weight, all_queries))
    far_gate, far_up, far_down = (other_core(w) for w in after[:3])
    parts = exchange(partial, XY)
    heads = exchange(project(parts, weight_t), ("z",))
    gain = lax.dynamic_slice_in_dim(norm_gain, depth * SLICE, SLICE, 0)[None]
    stream, chunks = pack(heads, own, gain, main, over, spread)
    arrived = exchange(chunks.reshape(NZ * PLANE, MAIN, CHUNK), ZXY).reshape(NZ, RCV, CHUNK)
    answers = experts(arrived, gate_weight, far_gate, up_weight, far_up, down_weight, far_down)
    returned = exchange(answers.reshape(NZ * PLANE, MAIN, CHUNK), ZXY).reshape(NZ, RCV, CHUNK)
    layer = combine(returned, stream, mix)
    final = exchange(layer.reshape(NZ, tok, SLICE), ("z",))
    return jnp.transpose(final, (1, 0, 2)).reshape(tok, D)


def solution(mesh):
    split = Mesh(mesh.devices.reshape(4, 2, 2, 2, NZ), ("y", "xh", "xl", "c", "z"))
    dp = ("y", "xh", "xl", "c")
    rows = dp + ("z",)
    placed = (
        P(rows, None),
        P(dp, "z"),
        P(dp, "z"),
        P(dp, "z"),
        P(dp, "z"),
        P(dp, "z"),
        P("z", dp),
        P(),
        P(rows, None),
        P(rows, None),
        P(None, rows),
        P(None, rows),
        P(rows, None),
    )
    return jax.shard_map(body, mesh=split, in_specs=placed, out_specs=P(rows, None), check_vma=False)
```

```python
import functools
import math

import jax
import jax.numpy as jnp
from jax import lax
from jax.experimental import pallas as pl
from jax.experimental.pallas import tpu as pltpu
from jax.sharding import Mesh, PartitionSpec as P

D = 4608
HD = 128
HEADS = 5
E = 8
TOP = 2
CAP = 5
NZ = 4
PLANE = 16
Q_DEV = 64
SLICE = D // NZ
MAIN = 16
OVER = NZ * CAP - MAIN
THIRD = SLICE // 3
CHUNK = SLICE + THIRD
PACK = 128
LINES = HEADS * Q_DEV + 8
NORM_EPS = 1e-06
NEGATIVE = -1e30
TO_BASE2 = math.log2(math.e) / math.sqrt(HD)

XY = ("y", "xh", "xl")
ZXY = ("z", "y", "xh", "xl")
F32 = jnp.float32
BF16 = jnp.bfloat16


VMEM = pl.BlockSpec(memory_space=pltpu.VMEM)
HBM = pl.BlockSpec(memory_space=pltpu.HBM)
ANY = pl.BlockSpec(memory_space=pl.ANY)


def params(mib):
    return pltpu.CompilerParams(vmem_limit_bytes=mib * 2**20)


def exchange(block, axes):
    return lax.all_to_all(block, axes, split_axis=0, concat_axis=0, tiled=True)


def other_core(block):
    return lax.ppermute(block, "c", [(0, 1), (1, 0)])


def around_z(blocks, depth):
    take = lambda a, i: lax.dynamic_index_in_dim(a, i % NZ, 0, keepdims=False)
    got = [take(blocks, depth)]
    for step in range(1, NZ):
        route = [(i, (i + step) % NZ) for i in range(NZ)]
        got.append(lax.ppermute(take(blocks, depth + step), "z", route))
    got = jnp.stack(got)
    return jnp.stack([take(got, depth - i + NZ) for i in range(NZ)])


def three_parts(value):
    high = value.astype(BF16).astype(F32)
    rest = value - high
    middle = rest.astype(BF16).astype(F32)
    return high, middle, (rest - middle).astype(BF16).astype(F32)


def dot_nt(a, b, **kw):
    return lax.dot_general(a, b, (((1,), (1,)), ((), ())), preferred_element_type=F32, **kw)


def dot_nn(a, b, **kw):
    return lax.dot_general(a, b, (((1,), (0,)), ((), ())), preferred_element_type=F32, **kw)


Q_BLOCKS = 8


def attend_kernel(place_ref, q_ref, ka_ref, kb_ref, na_ref, nb_ref, va_ref, vb_ref, wa_ref, wb_ref, out_ref):
    core, mine = place_ref[0], place_ref[1]
    rows = Q_BLOCKS * Q_DEV
    row = lax.broadcasted_iota(jnp.int32, (rows, HD), 0)
    lane = lax.broadcasted_iota(jnp.int32, (rows, HD), 1)
    block = pl.program_id(0) * Q_BLOCKS + row // Q_DEV
    q_pos = (block * 2 + core) * Q_DEV + row % Q_DEV
    k_pos = jnp.where(lane < Q_DEV, mine * Q_DEV + lane, (mine + 1 - 2 * core) * Q_DEV + lane - Q_DEV)
    allowed = k_pos <= q_pos
    pack = jnp.zeros((rows, PACK), F32)
    group = row % Q_DEV // 8 * 16
    for h in range(HEADS):
        cols = slice(h * HD, (h + 1) * HD)
        q = q_ref[:, :, cols].reshape(rows, HD)
        s1 = dot_nt(q, ka_ref[:, cols])
        s2 = dot_nt(q, kb_ref[:, cols])
        fresh = jnp.concatenate([na_ref[:, cols], nb_ref[:, cols]], axis=0)
        s3 = jnp.where(allowed, dot_nt(q, fresh), NEGATIVE)
        top = jnp.maximum(
            jnp.maximum(jnp.max(s1, axis=1, keepdims=True), jnp.max(s2, axis=1, keepdims=True)),
            jnp.max(s3, axis=1, keepdims=True),
        ) * TO_BASE2
        w1 = jnp.exp2(s1 * TO_BASE2 - top)
        w2 = jnp.exp2(s2 * TO_BASE2 - top)
        w3 = jnp.exp2(s3 * TO_BASE2 - top)
        total = (
            jnp.sum(w1, axis=1, keepdims=True)
            + jnp.sum(w2, axis=1, keepdims=True)
            + jnp.sum(w3, axis=1, keepdims=True)
        )
        fresh_v = jnp.concatenate([wa_ref[:, cols], wb_ref[:, cols]], axis=0)
        acc = (
            dot_nn(w1.astype(BF16), va_ref[:, cols])
            + dot_nn(w2.astype(BF16), vb_ref[:, cols])
            + dot_nn(w3.astype(BF16), fresh_v)
        )
        out_ref[:, h * Q_DEV : (h + 1) * Q_DEV, :] = (
            (acc / total).astype(BF16).reshape(Q_BLOCKS, Q_DEV, HD)
        )
        for part, value in enumerate(three_parts(top + jnp.log2(total))):
            pack = jnp.where(lane == group + part * HEADS + h, value, pack)
    folded = jnp.sum(pack.reshape(Q_BLOCKS, 8, 8, PACK), axis=1)
    out_ref[:, HEADS * Q_DEV :, :] = folded.astype(BF16)


def attend(place, q, *keys):
    whole = [pl.BlockSpec(a.shape, lambda i: (0, 0)) for a in keys]
    return pl.pallas_call(
        attend_kernel,
        grid=(PLANE // Q_BLOCKS,),
        out_shape=jax.ShapeDtypeStruct((PLANE, LINES, HD), BF16),
        in_specs=[
            pl.BlockSpec(memory_space=pltpu.SMEM),
            pl.BlockSpec((Q_BLOCKS, Q_DEV, HEADS * HD), lambda i: (i, 0, 0)),
            *whole,
        ],
        out_specs=pl.BlockSpec((Q_BLOCKS, LINES, HD), lambda i: (i, 0, 0)),
        compiler_params=params(56),
        cost_estimate=pl.CostEstimate(flops=11 * 10**9, bytes_accessed=10**7, transcendentals=11 * 10**6),
        name="attend",
    )(place, q, *keys)


def merge(parts_ref, out_ref):
    count = parts_ref.shape[0]
    sums = [parts_ref[i, HEADS * Q_DEV :, :].astype(F32) for i in range(count)]
    sums = [
        s + pltpu.roll(s, PACK - HEADS, axis=1) + pltpu.roll(s, PACK - 2 * HEADS, axis=1) for s in sums
    ]
    for h in range(HEADS):
        logs = [
            jnp.concatenate([s[:, g * 16 + h : g * 16 + h + 1] for g in range(8)], axis=0) for s in sums
        ]
        top = functools.reduce(jnp.maximum, logs)
        shares = [jnp.exp2(v - top) for v in logs]
        total = functools.reduce(jnp.add, shares)
        acc = functools.reduce(
            jnp.add,
            [
                shares[i] * parts_ref[i, h * Q_DEV : (h + 1) * Q_DEV, :].astype(F32)
                for i in range(count)
            ],
        )
        out_ref[:, h * HD : (h + 1) * HD] = (acc / total).astype(BF16)


def project_kernel(parts_ref, weight_hbm, out_ref, attended_ref, weight_ref, sems):
    pieces = [
        pltpu.make_async_copy(
            weight_hbm.at[z * SLICE : (z + 1) * SLICE, :], weight_ref.at[z], sems.at[z]
        )
        for z in range(NZ)
    ]
    for piece in pieces:
        piece.start()
    merge(parts_ref, attended_ref)
    for z, piece in enumerate(pieces):
        piece.wait()
        out_ref[z] = dot_nt(attended_ref[...], weight_ref[z]).astype(BF16)


def project(parts, weight):
    width = HEADS * HD
    return pl.pallas_call(
        project_kernel,
        out_shape=jax.ShapeDtypeStruct((NZ, Q_DEV, SLICE), BF16),
        in_specs=[VMEM, HBM],
        out_specs=VMEM,
        scratch_shapes=[
            pltpu.VMEM((Q_DEV, width), BF16),
            pltpu.VMEM((NZ, SLICE, width), BF16),
            pltpu.SemaphoreType.DMA((NZ,)),
        ],
        compiler_params=params(56),
        cost_estimate=pl.CostEstimate(flops=4 * 10**8, bytes_accessed=8 * 10**6, transcendentals=0),
        name="project",
    )(parts, weight)


def earlier():
    i = lax.broadcasted_iota(jnp.int32, (Q_DEV, Q_DEV), 0)
    j = lax.broadcasted_iota(jnp.int32, (Q_DEV, Q_DEV), 1)
    return i, j


def pack_kernel(heads_ref, own_ref, gain_ref, main_ref, over_ref, spread_ref, stream_ref, chunk_ref, made_ref, sems):
    summed = heads_ref[0].astype(F32)
    for z in range(1, NZ):
        summed = summed + heads_ref[z].astype(F32)
    stream = (own_ref[:, :SLICE].astype(F32) + summed).astype(BF16)
    stream_ref[...] = stream
    stream_f = stream.astype(F32)
    squares = stream_f * stream_f
    scaled = (stream_f * gain_ref[...]).astype(BF16)
    main = dot_nn(main_ref[...], scaled).astype(BF16)
    over = jnp.zeros((E * MAIN, THIRD), F32)
    for t in range(3):
        over = over + dot_nn(over_ref[t], scaled[:, t * THIRD : (t + 1) * THIRD])
    sums_row = dot_nt(jnp.ones((8, SLICE), F32), squares, precision=lax.Precision.HIGHEST)
    parts = jnp.concatenate(three_parts(sums_row), axis=0).astype(BF16)
    placed = dot_nt(parts, spread_ref[...])
    row = lax.broadcasted_iota(jnp.int32, (MAIN, HD), 0)
    for e in range(E):
        lanes = slice(e * HD, (e + 1) * HD)
        high, middle, low = placed[0:1, lanes], placed[8:9, lanes], placed[16:17, lanes]
        extra = jnp.where(
            row == 3 * OVER,
            high,
            jnp.where(row == 3 * OVER + 1, middle, jnp.where(row == 3 * OVER + 2, low, 0.0)),
        )
        here = slice(e * MAIN, (e + 1) * MAIN)
        begin = (over[here, :HD] + extra).astype(BF16)
        rest = over[here, HD:].astype(BF16)
        made_ref[e, :, :SLICE] = main[here]
        made_ref[e, :, SLICE : SLICE + HD] = begin
        made_ref[e, :, SLICE + HD :] = rest
    copies = [
        pltpu.make_async_copy(made_ref, chunk_ref.at[z, :, x], sems.at[z, x])
        for z in range(NZ)
        for x in range(2)
    ]
    for copy in copies:
        copy.start()
    for copy in copies:
        copy.wait()


def pack(heads, own, gain, main, over, spread):
    return pl.pallas_call(
        pack_kernel,
        out_shape=(
            jax.ShapeDtypeStruct((Q_DEV, SLICE), BF16),
            jax.ShapeDtypeStruct((NZ, E, 2, MAIN, CHUNK), BF16),
        ),
        in_specs=[VMEM] * 6,
        out_specs=(VMEM, HBM),
        scratch_shapes=[pltpu.VMEM((E, MAIN, CHUNK), BF16), pltpu.SemaphoreType.DMA((NZ, 2))],
        compiler_params=params(40),
        cost_estimate=pl.CostEstimate(flops=3 * 10**7, bytes_accessed=5 * 10**6, transcendentals=0),
        name="pack",
    )(heads, own, gain, main, over, spread)


RCV = PLANE * MAIN
F_BLOCK = 256
EXT = PLANE * OVER
ALL = RCV + EXT
def iotas(rows, cols):
    return (
        lax.broadcasted_iota(jnp.int32, (rows, cols), 0),
        lax.broadcasted_iota(jnp.int32, (rows, cols), 1),
    )


def unpack(x_ref, rows_ref):
    over_row, line = iotas(EXT, RCV)
    extra_sum = jnp.zeros((RCV, HD), F32)
    for z in range(NZ):
        rows_ref[:RCV, z * SLICE : (z + 1) * SLICE] = x_ref[z, :, :SLICE]
        over = x_ref[z, :, SLICE:]
        extra_sum = extra_sum + over[:, :HD].astype(F32)
        for t in range(3):
            pick = (line // MAIN == over_row // OVER) & (line % MAIN == t * OVER + over_row % OVER)
            rows_ref[RCV:, z * SLICE + t * THIRD : z * SLICE + (t + 1) * THIRD] = dot_nn(
                jnp.where(pick, 1.0, 0.0).astype(BF16), over
            ).astype(BF16)

    source, line = iotas(PLANE, RCV)
    part = line % MAIN
    pick = (line // MAIN == source) & (part >= 3 * OVER) & (part < 3 * OVER + 3)
    sums = dot_nn(jnp.where(pick, 1.0, 0.0), extra_sum, precision=lax.Precision.HIGHEST)
    row, source = iotas(ALL, PLANE)
    owner = jnp.where(row < RCV, row // MAIN, (row - RCV) // OVER)
    spread = dot_nn(jnp.where(owner == source, 1.0, 0.0), sums, precision=lax.Precision.HIGHEST)
    row, lane = iotas(ALL, HD)
    slot = jnp.where(row < RCV, row % MAIN, MAIN + (row - RCV) % OVER)
    column = jnp.sum(jnp.where(lane == slot, spread, 0.0), axis=1, keepdims=True)
    return lax.rsqrt(column * (1.0 / D) + NORM_EPS)


def repack(answer, made_ref, z):
    width = answer.shape[1]
    made_ref[z, :, :width] = answer[:RCV]
    line, over_row = iotas(RCV, EXT)
    for third in range(width // THIRD):
        over = jnp.zeros((RCV, HD), F32)
        for t in range(3):
            pick = (line // MAIN == over_row // OVER) & (line % MAIN == t * OVER + over_row % OVER)
            at = third * THIRD + t * HD
            over = over + dot_nn(jnp.where(pick, 1.0, 0.0).astype(BF16), answer[RCV:, at : at + HD])
        made_ref[z, :, width + third * HD : width + (third + 1) * HD] = over.astype(BF16)


AHEAD = 2
SLOTS = AHEAD + 1


def experts_kernel(
    x_any, ga_hbm, gb_hbm, ua_hbm, ub_hbm, da_hbm, db_hbm, out_hbm,
    made_ref, rows_ref, scale_ref, hidden_ref, both_ref, down_ref, x_sem, weight_sem, down_sem, out_sem,
):
    half = da_hbm.shape[0]
    steps = half // F_BLOCK

    def weight_copies(step, gate_hbm, up_hbm, block):
        cols = pl.ds(pl.multiple_of(block * F_BLOCK, F_BLOCK), F_BLOCK)
        slot = lax.rem(step, SLOTS)
        return (
            pltpu.make_async_copy(gate_hbm.at[:, cols], both_ref.at[slot, :, :F_BLOCK], weight_sem.at[0, slot]),
            pltpu.make_async_copy(up_hbm.at[:, cols], both_ref.at[slot, :, F_BLOCK:], weight_sem.at[1, slot]),
        )

    def down_copies():
        return [
            [
                pltpu.make_async_copy(
                    hbm.at[:, z * SLICE : (z + 1) * SLICE],
                    down_ref.at[z, side * half : (side + 1) * half, :],
                    down_sem.at[side, z],
                )
                for side, hbm in enumerate((da_hbm, db_hbm))
            ]
            for z in range(NZ)
        ]

    arrive = pltpu.make_async_copy(x_any, made_ref, x_sem)
    arrive.start()
    arrive.wait()
    for step in range(AHEAD):
        for copy in weight_copies(step, ga_hbm, ua_hbm, step):
            copy.start()
    scale_ref[...] = jnp.broadcast_to(unpack(made_ref, rows_ref), (ALL, HD))

    @pl.loop(0, 2 * steps)
    def _(step):
        later = step + AHEAD

        @pl.when(later < steps)
        def _():
            for copy in weight_copies(later, ga_hbm, ua_hbm, later):
                copy.start()

        @pl.when((later >= steps) & (later < 2 * steps))
        def _():
            for copy in weight_copies(later, gb_hbm, ub_hbm, later - steps):
                copy.start()

        @pl.when(later == 2 * steps)
        def _():
            for pair in down_copies():
                for copy in pair:
                    copy.start()

        for copy in weight_copies(step, ga_hbm, ua_hbm, 0):
            copy.wait()
        slot = lax.rem(step, SLOTS)
        both = dot_nn(rows_ref[...], both_ref[slot]) * scale_ref[:, :1]
        gate, up = both[:, :F_BLOCK], both[:, F_BLOCK:]
        to = pl.ds(pl.multiple_of(step * F_BLOCK, F_BLOCK), F_BLOCK)
        hidden_ref[:, to] = (gate / (1.0 + jnp.exp(-gate)) * up).astype(BF16)

    sent = []
    for z, pair in enumerate(down_copies()):
        for copy in pair:
            copy.wait()
        repack(dot_nn(hidden_ref[...], down_ref[z]).astype(BF16), made_ref, z)
        sent.append(pltpu.make_async_copy(made_ref.at[z], out_hbm.at[z], out_sem.at[z]))
        sent[-1].start()
    for copy in sent:
        copy.wait()


def experts(x, ga, gb, ua, ub, da, db):
    width = ga.shape[1]
    return pl.pallas_call(
        experts_kernel,
        out_shape=jax.ShapeDtypeStruct(x.shape, BF16),
        in_specs=[ANY] + [HBM] * 6,
        out_specs=HBM,
        scratch_shapes=[
            pltpu.VMEM(x.shape, BF16),
            pltpu.VMEM((ALL, D), BF16),
            pltpu.VMEM((ALL, HD), F32),
            pltpu.VMEM((ALL, 2 * width), BF16),
            pltpu.VMEM((SLOTS, D, 2 * F_BLOCK), BF16),
            pltpu.VMEM((NZ, 2 * width, SLICE), BF16),
            pltpu.SemaphoreType.DMA,
            pltpu.SemaphoreType.DMA((2, SLOTS)),
            pltpu.SemaphoreType.DMA((2, NZ)),
            pltpu.SemaphoreType.DMA((NZ,)),
        ],
        compiler_params=params(56),
        cost_estimate=pl.CostEstimate(flops=14 * 10**9, bytes_accessed=48 * 10**6, transcendentals=10**6),
        name="experts",
    )(x, ga, gb, ua, ub, da, db)


def place_rows(codes, main_ref, over_ref, spread_ref):
    kind, lane = iotas(8, PACK)
    turned = dot_nt(jnp.where(kind == lane, 1.0, 0.0).astype(BF16), codes)
    first, second = turned[0:1, :], turned[1:2, :]
    expert = lax.broadcasted_iota(jnp.int32, (E, Q_DEV), 0).astype(F32)
    hot0 = jnp.where(expert == first, 1.0, 0.0)
    hot1 = jnp.where(expert == second, 1.0, 0.0)
    j, i = earlier()
    before_t = jnp.where((j < i) & (j // 16 == i // 16), 1.0, 0.0)
    counts = dot_nn((hot0 + hot1).astype(BF16), before_t.astype(BF16))
    base = (lax.broadcasted_iota(jnp.int32, (1, Q_DEV), 1) // 16 * CAP).astype(F32)
    slot0 = jnp.sum(counts * hot0, axis=0, keepdims=True) + base
    slot1 = jnp.sum(counts * hot1, axis=0, keepdims=True) + base

    def placing(slot, which):
        hit = ((slot == slot0) & (which == first)) | ((slot == slot1) & (which == second))
        return jnp.where(hit, 1.0, 0.0).astype(BF16)

    line = lax.broadcasted_iota(jnp.int32, (E * MAIN, Q_DEV), 0)
    which = (line // MAIN).astype(F32)
    part = line % MAIN
    main_ref[...] = placing(part.astype(F32), which)
    for t in range(3):
        over_ref[t] = placing(jnp.where(part // OVER == t, MAIN + part % OVER, -1).astype(F32), which)
    line = lax.broadcasted_iota(jnp.int32, (E * HD, Q_DEV), 0)
    spread_ref[...] = placing((line % HD).astype(F32), (line // HD).astype(F32))


def routing_kernel(own_ref, main_ref, over_ref, spread_ref, mix_ref):
    codes = own_ref[:, SLICE:]
    place_rows(codes, main_ref, over_ref, spread_ref)
    routes_ref = codes.astype(F32)
    first, second = routes_ref[:, 0:1], routes_ref[:, 1:2]
    weight0 = routes_ref[:, 2:3] + routes_ref[:, 3:4] + routes_ref[:, 4:5]
    weight1 = routes_ref[:, 5:6] + routes_ref[:, 6:7] + routes_ref[:, 7:8]
    expert = lax.broadcasted_iota(jnp.int32, (Q_DEV, HD), 1).astype(F32)
    hot0 = jnp.where(expert == first, 1.0, 0.0)
    hot1 = jnp.where(expert == second, 1.0, 0.0)
    i, j = earlier()
    before = jnp.where((j < i) & (j // 16 == i // 16), 1.0, 0.0)
    counts = dot_nn(before.astype(BF16), (hot0 + hot1).astype(BF16))
    base = (lax.broadcasted_iota(jnp.int32, (Q_DEV, 1), 0) // 16 * CAP).astype(F32)
    slot0 = jnp.sum(counts * hot0, axis=1, keepdims=True) + base
    slot1 = jnp.sum(counts * hot1, axis=1, keepdims=True) + base
    col = lax.broadcasted_iota(jnp.int32, (Q_DEV, RCV), 1)
    part = col % MAIN
    which = (col // (2 * MAIN)).astype(F32)
    for kind in range(4):
        slot = part if kind == 0 else jnp.where(part // OVER == kind - 1, MAIN + part % OVER, -1)
        slot = slot.astype(F32)
        mix = jnp.where((slot == slot0) & (which == first), weight0, 0.0) + jnp.where(
            (slot == slot1) & (which == second), weight1, 0.0
        )
        for at, value in enumerate(three_parts(mix)):
            mix_ref[kind, at * Q_DEV : (at + 1) * Q_DEV, :] = value.astype(BF16)


def routing(own):
    return pl.pallas_call(
        routing_kernel,
        out_shape=(
            jax.ShapeDtypeStruct((E * MAIN, Q_DEV), BF16),
            jax.ShapeDtypeStruct((3, E * MAIN, Q_DEV), BF16),
            jax.ShapeDtypeStruct((E * HD, Q_DEV), BF16),
            jax.ShapeDtypeStruct((4, 3 * Q_DEV, RCV), BF16),
        ),
        compiler_params=params(30),
        cost_estimate=pl.CostEstimate(flops=10**6, bytes_accessed=10**6, transcendentals=0),
        name="routing",
    )(own)


def combine_kernel(returned_hbm, stream_ref, mix_ref, out_ref, returned_ref, sems):
    copies = [
        pltpu.make_async_copy(returned_hbm.at[z], returned_ref.at[z], sems.at[z]) for z in range(NZ)
    ]
    for copy in copies:
        copy.start()

    def fold(kind, block):
        moved = dot_nn(mix_ref[kind], block)
        return moved[:Q_DEV] + moved[Q_DEV : 2 * Q_DEV] + moved[2 * Q_DEV :]

    total = stream_ref[...].astype(F32)
    extra = [jnp.zeros((Q_DEV, HD), F32)] * (SLICE // HD)
    for z in range(NZ):
        copies[z].wait()
        total = total + fold(0, returned_ref[z, :, :SLICE])
        for at in range(SLICE // HD):
            lanes = slice(SLICE + at // 3 * HD, SLICE + (at // 3 + 1) * HD)
            extra[at] = extra[at] + fold(at % 3 + 1, returned_ref[z, :, lanes])
    for at, part in enumerate(extra):
        cols = slice(at * HD, (at + 1) * HD)
        out_ref[:, cols] = (total[:, cols] + part).astype(BF16)


def combine(returned, stream, mix):
    return pl.pallas_call(
        combine_kernel,
        out_shape=jax.ShapeDtypeStruct((Q_DEV, SLICE), BF16),
        in_specs=[ANY, VMEM, VMEM],
        out_specs=VMEM,
        scratch_shapes=[pltpu.VMEM(returned.shape, BF16), pltpu.SemaphoreType.DMA((NZ,))],
        compiler_params=params(40),
        cost_estimate=pl.CostEstimate(flops=7 * 10**8, bytes_accessed=5 * 10**6, transcendentals=0),
        name="combine",
    )(returned, stream, mix)


def body(
    residual,
    queries,
    new_keys,
    new_values,
    cache_keys,
    cache_values,
    out_weight,
    norm_gain,
    route_ids,
    route_weight,
    gate_weight,
    up_weight,
    down_weight,
):
    core = lax.axis_index("c")
    mine = lax.axis_index(XY) * 2 + core
    depth = lax.axis_index("z")

    head_width = HEADS * HD
    far_keys = other_core(cache_keys)
    far_values = other_core(cache_values)
    far_new_keys = other_core(new_keys)
    far_new_values = other_core(new_values)
    weight_t = lax.all_gather(out_weight.T, XY + ("c",), axis=0, tiled=True)
    all_queries = exchange(jnp.broadcast_to(queries[None], (PLANE, Q_DEV, head_width)), XY)
    tok = residual.shape[0]
    codes = jnp.concatenate(
        [
            route_ids.astype(F32),
            jnp.stack(three_parts(route_weight[:, 0]) + three_parts(route_weight[:, 1]), axis=1),
        ],
        axis=1,
    ).astype(BF16)
    codes = jnp.pad(codes, ((0, 0), (0, PACK - codes.shape[1])))
    own = jnp.transpose(residual.reshape(tok, NZ, SLICE), (1, 0, 2))
    own = jnp.concatenate([own, jnp.broadcast_to(codes[None], (NZ, tok, PACK))], axis=2)
    own = around_z(own, depth).reshape(Q_DEV, SLICE + PACK)
    main, over, spread, mix = routing(own)
    mix, all_queries = lax.optimization_barrier((mix, all_queries))

    place = jnp.stack([core, mine]).astype(jnp.int32)
    partial = attend(
        place, all_queries, cache_keys, far_keys, new_keys, far_new_keys,
        cache_values, far_values, new_values, far_new_values,
    )
    after = lax.optimization_barrier((gate_weight, up_weight, down_weight, all_queries))
    far_gate, far_up, far_down = (other_core(w) for w in after[:3])
    parts = exchange(partial, XY)
    heads = exchange(project(parts, weight_t), ("z",))
    gain = lax.dynamic_slice_in_dim(norm_gain, depth * SLICE, SLICE, 0)[None]
    stream, chunks = pack(heads, own, gain, main, over, spread)
    arrived = exchange(chunks.reshape(NZ * PLANE, MAIN, CHUNK), ZXY).reshape(NZ, RCV, CHUNK)
    answers = experts(arrived, gate_weight, far_gate, up_weight, far_up, down_weight, far_down)
    returned = exchange(answers.reshape(NZ * PLANE, MAIN, CHUNK), ZXY).reshape(NZ, RCV, CHUNK)
    layer = combine(returned, stream, mix)
    final = exchange(layer.reshape(NZ, tok, SLICE), ("z",))
    return jnp.transpose(final, (1, 0, 2)).reshape(tok, D)


def solution(mesh):
    split = Mesh(mesh.devices.reshape(4, 2, 2, 2, NZ), ("y", "xh", "xl", "c", "z"))
    dp = ("y", "xh", "xl", "c")
    rows = dp + ("z",)
    placed = (
        P(rows, None),
        P(dp, "z"),
        P(dp, "z"),
        P(dp, "z"),
        P(dp, "z"),
        P(dp, "z"),
        P("z", dp),
        P(),
        P(rows, None),
        P(rows, None),
        P(None, rows),
        P(None, rows),
        P(rows, None),
    )
    return jax.shard_map(body, mesh=split, in_specs=placed, out_specs=P(rows, None), check_vma=False)
```
